32 devices in a mesh: book: 2 (over y), trade: 8 (over z, x), path: 2 (over core).
Axes of the slice: x: 2, y: 2, z: 4, core: 2. Of those that a mesh axis runs over, the one named last changes fastest.
Arguments:
- shocks: float32 [4, 2, 2, 8], P('book', None, 'path', 'trade'), parts along dimension 0, may hold values from -6 to 6
- trade_kind: int32 [8192, 16], P(('book', 'trade')), parts along dimension 0, may hold values from 0 to 2
- cash_start: int32 [8192, 16], P(('book', 'trade')), parts along dimension 0, may hold values from 3 to 34
- cash_count: int32 [8192, 16], P(('book', 'trade')), parts along dimension 0, may hold values from 4 to 63
- strike: float32 [8192, 16], P(('book', 'trade')), parts along dimension 0, may hold values from 0.005 to 0.05
- normal_vol: float32 [8192, 16], P(('book', 'trade')), parts along dimension 0, may hold values from 0.004 to 0.015
- notional: float32 [8192, 16], P(('book', 'trade')), parts along dimension 0, may hold values from -4 to 4
- block_count: int32 [8192], P(('book', 'trade')), parts along dimension 0, may hold values from 1 to 16
- block_set: int32 [8192], P(('book', 'trade')), parts along dimension 0, may hold values from 0 to 255, as said below
Outputs:
- exposure: float32 [512, 2, 16], P(('book', 'trade'), None, 'path'), parts along dimension 0
The draws below stay inside these ranges and needn't reach their ends.
There are 2 independent parts, one for each index of `book`. The reference program is written for one: setup_inputs(seed, part) draws one part's arguments, and reference() takes and returns one part's arrays. A program takes and returns all parts, laid end to end along the dimension named above; each array names one. Nothing has to cross between parts.
Inputs may be any that keep to these rules, and one draw needn't show every extreme that they name: `block_set`: trade block b has its netting set s with s // 32 == (b % 512) // 64: the blocks of one device are ordered by the device that owns their set, 64 blocks to each.
All inputs are finite; a program needn't handle non-finite values.
Results may differ from the reference program's by a relative error of at most 0.0003.
Values sent between devices are 32-bit elements; how exact they have to be, the bound alone decides.
No kernel may reach another device: no remote copies, remote signals or barrier semaphores. Data moves between devices by JAX's collectives and lax.ppermute only.
A program may use at most 64 MiB of HBM per device.

```python
import math
import jax
import jax.numpy as jnp
from jax import lax

GRID = 128
DATES = 2
SLOTS = 16
BLK_DEV = 512
SET_DEV = 32
P_LOC = 8
PATHS = 16
BLK_OWNER = 64
BLOCKS = 4096
SETS = 256
N_PATH = 2


def draw_block_set(key, part):
    key = jax.random.fold_in(key, 7)
    within = jax.random.randint(key, (BLOCKS,), 0, SET_DEV)
    owner = jnp.arange(BLOCKS, dtype=jnp.int32) % BLK_DEV // BLK_OWNER
    return (owner * SET_DEV + within).astype(jnp.int32)


def plant(values, key, low, top_value):
    spot = [jax.random.randint(jax.random.fold_in(key, axis), (), 0, length) for axis, length in enumerate(values.shape)]
    longest = values.shape.index(max(values.shape))
    next_to = spot[:longest] + [(spot[longest] + 1) % values.shape[longest]] + spot[longest + 1:]
    return values.at[tuple(spot)].set(low).at[tuple(next_to)].set(top_value)


def block_levels(rng, dims, pieces, least, largest):
    gain, own = 1.0, jax.random.fold_in(rng, 6)
    for axis_at, parts in pieces:
        steps = jnp.exp(jax.random.uniform(jax.random.fold_in(own, axis_at), (parts,), jnp.float32, least / len(pieces), largest / len(pieces)))
        gain = gain * jnp.repeat(steps, dims[axis_at] // parts).reshape([-1 if axis == axis_at else 1 for axis in range(len(dims))])
    return gain


def bell_draw(stream_key, extent, scale, bound, split=(), kind=jnp.bfloat16):
    values = jax.random.normal(stream_key, extent, jnp.float32) * scale
    if len(split) > 0:
        values = block_levels(stream_key, extent, split, -0.22, 0.18) * values
    return jnp.clip(values, min=-bound, max=bound).astype(kind)


def setup_inputs(seed: int = 0, part: int = 0) -> dict:
    streams_of = jax.random.split(jax.random.key(seed), 10)
    part_splits = jax.random.split(jax.random.fold_in(streams_of[9], part), 10)
    shocks = bell_draw(part_splits[0], (2, DATES, N_PATH, P_LOC), 1.0, 6.0, ((2, 2), (3, 8)), jnp.float32)
    trade_kind = plant(jax.random.randint(part_splits[1], (BLOCKS, SLOTS), 0, 3), jax.random.fold_in(part_splits[1], 1), 0, 2).astype(jnp.int32)
    cash_start = plant(jax.random.randint(part_splits[2], (BLOCKS, SLOTS), DATES + 1, DATES + 1 + GRID // 4), jax.random.fold_in(part_splits[2], 1), DATES + 1, (DATES + 1 + GRID // 4) - 1).astype(jnp.int32)
    cash_count = plant(jax.random.randint(part_splits[3], (BLOCKS, SLOTS), 4, GRID // 2), jax.random.fold_in(part_splits[3], 1), 4, (GRID // 2) - 1).astype(jnp.int32)
    strike = jnp.clip(0.005 + 0.045 * jax.random.uniform(part_splits[4], (BLOCKS, SLOTS), jnp.float32) ** block_levels(part_splits[4], (BLOCKS, SLOTS), ((0, 8),), -0.2, 0.2), 0.005, 0.05)
    normal_vol = jnp.clip(jnp.exp(math.log(0.015) - 1.3217558 * jax.random.uniform(part_splits[5], (BLOCKS, SLOTS), jnp.float32) ** block_levels(part_splits[5], (BLOCKS, SLOTS), ((0, 8),), -0.2, 0.2)), 0.004, 0.015)
    notional = bell_draw(part_splits[6], (BLOCKS, SLOTS), 1.0, 4.0, ((0, 8),), jnp.float32)
    block_count = plant(jax.random.randint(part_splits[7], (BLOCKS,), 1, SLOTS + 1), jax.random.fold_in(part_splits[7], 1), 1, SLOTS).astype(jnp.int32)
    block_set = draw_block_set(jax.random.fold_in(jax.random.fold_in(streams_of[9], part), 71), part)
    return {"shocks": shocks, "trade_kind": trade_kind, "cash_start": cash_start, "cash_count": cash_count, "strike": strike, "normal_vol": normal_vol, "notional": notional, "block_count": block_count, "block_set": block_set}


YEAR_STEP = 0.25
FLAT_RATE = 0.03
REVERT_FAST = 0.5
REVERT_SLOW = 0.04
VOL_FAST = 0.012
VOL_SLOW = 0.009
FACTOR_CORR = -0.6
HIGHEST = lax.Precision.HIGHEST

def loading(reversion, horizon):
    return (1.0 - jnp.exp(-reversion * horizon)) / reversion

def one_variance(reversion, volatility, horizon):
    return volatility ** 2 / reversion ** 2 * (horizon + 2.0 / reversion * jnp.exp(-reversion * horizon) - 0.5 / reversion * jnp.exp(-2.0 * reversion * horizon) - 1.5 / reversion)

def factor_variance(horizon):
    fast_part = one_variance(REVERT_FAST, VOL_FAST, horizon)
    slow_part = one_variance(REVERT_SLOW, VOL_SLOW, horizon)
    both_rates = REVERT_FAST + REVERT_SLOW
    cross_part = 2.0 * FACTOR_CORR * VOL_FAST * VOL_SLOW / (REVERT_FAST * REVERT_SLOW) * (horizon + (jnp.exp(-REVERT_FAST * horizon) - 1.0) / REVERT_FAST + (jnp.exp(-REVERT_SLOW * horizon) - 1.0) / REVERT_SLOW - (jnp.exp(-both_rates * horizon) - 1.0) / both_rates)
    return fast_part + slow_part + cross_part

def evolve(path_shocks):
    fast_keep = math.exp(-REVERT_FAST * YEAR_STEP)
    slow_keep = math.exp(-REVERT_SLOW * YEAR_STEP)
    fast_scale = VOL_FAST * math.sqrt((1.0 - math.exp(-2.0 * REVERT_FAST * YEAR_STEP)) / (2.0 * REVERT_FAST))
    slow_scale = VOL_SLOW * math.sqrt((1.0 - math.exp(-2.0 * REVERT_SLOW * YEAR_STEP)) / (2.0 * REVERT_SLOW))
    mixing = math.sqrt(1.0 - FACTOR_CORR ** 2)
    fast_state = jnp.zeros(path_shocks.shape[2:], jnp.float32)
    slow_state = jnp.zeros(path_shocks.shape[2:], jnp.float32)
    fast_path = []
    slow_path = []
    for period in range(path_shocks.shape[1]):
        fast_state = fast_state * fast_keep + fast_scale * path_shocks[0, period]
        slow_state = slow_state * slow_keep + slow_scale * (FACTOR_CORR * path_shocks[0, period] + mixing * path_shocks[1, period])
        fast_path.append(fast_state)
        slow_path.append(slow_state)
    return jnp.stack([jnp.stack(fast_path), jnp.stack(slow_path)])

def discount_table(states):
    dates_count = states.shape[1]
    maturity = lax.broadcasted_iota(jnp.int32, (GRID, 1, 1), 0).astype(jnp.float32) * YEAR_STEP
    valued = (lax.broadcasted_iota(jnp.int32, (1, dates_count, 1), 1) + 1).astype(jnp.float32) * YEAR_STEP
    horizon = maturity - valued
    log_front = -FLAT_RATE * horizon + 0.5 * (factor_variance(horizon) - factor_variance(maturity) + factor_variance(valued))
    return jnp.exp(log_front - loading(REVERT_FAST, horizon) * states[0][None] - loading(REVERT_SLOW, horizon) * states[1][None])

def price_blocks(trade_kind, cash_start, cash_count, strike, normal_vol, notional, block_count, discounts, dates_count):
    groups, slot_count = cash_start.shape
    cash_nodes = lax.broadcasted_iota(jnp.int32, (1, 1, GRID), 2)
    first_node = cash_start[:, :, None]
    last_node = (cash_start + cash_count)[:, :, None]
    accrual = jnp.where((cash_nodes > first_node) & (cash_nodes <= last_node), YEAR_STEP, 0.0).astype(jnp.float32)
    endpoints = (jnp.where(cash_nodes == first_node, 1.0, 0.0) - jnp.where(cash_nodes == last_node, 1.0, 0.0)).astype(jnp.float32)
    weights = jnp.concatenate([accrual, endpoints], axis=0).reshape(2 * groups * slot_count, GRID)
    products = jnp.dot(weights, discounts, precision=HIGHEST, preferred_element_type=jnp.float32)
    products = products.reshape(2, groups, slot_count, dates_count, -1)
    annuity = products[0]
    float_leg = products[1]
    swap_rate = float_leg / annuity
    valued = (lax.broadcasted_iota(jnp.int32, (1, 1, dates_count, 1), 2) + 1).astype(jnp.float32) * YEAR_STEP
    expiry = cash_start.astype(jnp.float32)[:, :, None, None] * YEAR_STEP
    spread = normal_vol[:, :, None, None] * jnp.sqrt(expiry - valued)
    moneyness = swap_rate - strike[:, :, None, None]
    standard = moneyness / spread
    normal_cdf = 0.5 * (1.0 + jax.scipy.special.erf(standard * (1.0 / math.sqrt(2.0))))
    normal_pdf = jnp.exp(-0.5 * standard * standard) * (1.0 / math.sqrt(2.0 * math.pi))
    offset = jnp.where(trade_kind == 1, 1.0, jnp.where(trade_kind == 2, 0.5, 0.0))[:, :, None, None]
    factor = (jnp.where(trade_kind == 2, 2.0, 1.0) * notional)[:, :, None, None]
    trade_value = factor * annuity * (moneyness * (normal_cdf - offset) + spread * normal_pdf)
    occupied = lax.broadcasted_iota(jnp.int32, (groups, slot_count), 1) < block_count[:, None]
    trade_value = jnp.where(occupied[:, :, None, None], trade_value, 0.0)
    return lax.optimization_barrier(jnp.sum(trade_value, axis=1)).reshape(groups, -1)

def reference(shocks, trade_kind, cash_start, cash_count, strike, normal_vol, notional, block_count, block_set):
    path_shocks = shocks.reshape(2, DATES, PATHS)
    discounts = discount_table(evolve(path_shocks)).reshape(GRID, DATES * PATHS)
    group_size = 256
    turns = BLOCKS // group_size

    def one_turn(running, turn_index):
        first_row = turn_index * group_size

        def window_of(array):
            return lax.dynamic_slice_in_dim(array, first_row, group_size, 0)
        totals = price_blocks(window_of(trade_kind), window_of(cash_start), window_of(cash_count), window_of(strike), window_of(normal_vol), window_of(notional), window_of(block_count), discounts, DATES)
        set_ids = window_of(block_set)
        return (running + jax.ops.segment_sum(totals, set_ids, num_segments=SETS), None)
    netted, _ = lax.scan(one_turn, jnp.zeros((SETS, DATES * PATHS), jnp.float32), jnp.arange(turns, dtype=jnp.int32))
    return jnp.maximum(netted, 0.0).reshape(SETS, DATES, PATHS)
```

```python
import math

import jax
import jax.numpy as jnp
from jax import lax
from jax.experimental import pallas as pl
from jax.experimental.pallas import tpu as pltpu
from jax.sharding import PartitionSpec as P

GRID = 128
SET_DEV = 32


YEAR_STEP = 0.25
FLAT_RATE = 0.03
REVERT_FAST = 0.5
REVERT_SLOW = 0.04
VOL_FAST = 0.012
VOL_SLOW = 0.009
FACTOR_CORR = -0.6
HIGHEST = lax.Precision.HIGHEST


def loading(reversion, horizon):
    return (1.0 - jnp.exp(-reversion * horizon)) / reversion


def one_variance(reversion, volatility, horizon):
    return (
        volatility**2
        / reversion**2
        * (
            horizon
            + 2.0 / reversion * jnp.exp(-reversion * horizon)
            - 0.5 / reversion * jnp.exp(-2.0 * reversion * horizon)
            - 1.5 / reversion
        )
    )


def factor_variance(horizon):
    fast_part = one_variance(REVERT_FAST, VOL_FAST, horizon)
    slow_part = one_variance(REVERT_SLOW, VOL_SLOW, horizon)
    both_rates = REVERT_FAST + REVERT_SLOW
    cross_part = (
        2.0
        * FACTOR_CORR
        * VOL_FAST
        * VOL_SLOW
        / (REVERT_FAST * REVERT_SLOW)
        * (
            horizon
            + (jnp.exp(-REVERT_FAST * horizon) - 1.0) / REVERT_FAST
            + (jnp.exp(-REVERT_SLOW * horizon) - 1.0) / REVERT_SLOW
            - (jnp.exp(-both_rates * horizon) - 1.0) / both_rates
        )
    )
    return fast_part + slow_part + cross_part


def evolve(path_shocks):
    fast_keep = math.exp(-REVERT_FAST * YEAR_STEP)
    slow_keep = math.exp(-REVERT_SLOW * YEAR_STEP)
    fast_scale = VOL_FAST * math.sqrt(
        (1.0 - math.exp(-2.0 * REVERT_FAST * YEAR_STEP)) / (2.0 * REVERT_FAST)
    )
    slow_scale = VOL_SLOW * math.sqrt(
        (1.0 - math.exp(-2.0 * REVERT_SLOW * YEAR_STEP)) / (2.0 * REVERT_SLOW)
    )
    mixing = math.sqrt(1.0 - FACTOR_CORR**2)
    fast_state = jnp.zeros(path_shocks.shape[2:], jnp.float32)
    slow_state = jnp.zeros(path_shocks.shape[2:], jnp.float32)
    fast_path = []
    slow_path = []
    for period in range(path_shocks.shape[1]):
        fast_state = fast_state * fast_keep + fast_scale * path_shocks[0, period]
        slow_state = slow_state * slow_keep + slow_scale * (
            FACTOR_CORR * path_shocks[0, period] + mixing * path_shocks[1, period]
        )
        fast_path.append(fast_state)
        slow_path.append(slow_state)
    return jnp.stack([jnp.stack(fast_path), jnp.stack(slow_path)])


def discount_table(states):
    dates_count = states.shape[1]
    maturity = lax.broadcasted_iota(jnp.int32, (GRID, 1, 1), 0).astype(jnp.float32) * YEAR_STEP
    valued = (lax.broadcasted_iota(jnp.int32, (1, dates_count, 1), 1) + 1).astype(
        jnp.float32
    ) * YEAR_STEP
    horizon = maturity - valued
    log_front = -FLAT_RATE * horizon + 0.5 * (
        factor_variance(horizon) - factor_variance(maturity) + factor_variance(valued)
    )
    return jnp.exp(
        log_front
        - loading(REVERT_FAST, horizon) * states[0][None]
        - loading(REVERT_SLOW, horizon) * states[1][None]
    )


def price_blocks(
    trade_kind,
    cash_start,
    cash_count,
    strike,
    normal_vol,
    notional,
    block_count,
    discounts,
    dates_count,
):
    groups, slot_count = cash_start.shape
    cash_nodes = lax.broadcasted_iota(jnp.int32, (1, 1, GRID), 2)
    first_node = cash_start[:, :, None]
    last_node = (cash_start + cash_count)[:, :, None]
    accrual = jnp.where(
        (cash_nodes > first_node) & (cash_nodes <= last_node), YEAR_STEP, 0.0
    ).astype(jnp.float32)
    endpoints = (
        jnp.where(cash_nodes == first_node, 1.0, 0.0) - jnp.where(cash_nodes == last_node, 1.0, 0.0)
    ).astype(jnp.float32)
    weights = jnp.concatenate([accrual, endpoints], axis=0).reshape(2 * groups * slot_count, GRID)
    products = jnp.dot(weights, discounts, precision=HIGHEST, preferred_element_type=jnp.float32)
    products = products.reshape(2, groups, slot_count, dates_count, -1)
    annuity = products[0]
    float_leg = products[1]
    swap_rate = float_leg / annuity
    valued = (lax.broadcasted_iota(jnp.int32, (1, 1, dates_count, 1), 2) + 1).astype(
        jnp.float32
    ) * YEAR_STEP
    expiry = cash_start.astype(jnp.float32)[:, :, None, None] * YEAR_STEP
    spread = normal_vol[:, :, None, None] * jnp.sqrt(expiry - valued)
    moneyness = swap_rate - strike[:, :, None, None]
    standard = moneyness / spread
    normal_cdf = 0.5 * (1.0 + jax.scipy.special.erf(standard * (1.0 / math.sqrt(2.0))))
    normal_pdf = jnp.exp(-0.5 * standard * standard) * (1.0 / math.sqrt(2.0 * math.pi))
    offset = jnp.where(trade_kind == 1, 1.0, jnp.where(trade_kind == 2, 0.5, 0.0))[:, :, None, None]
    factor = (jnp.where(trade_kind == 2, 2.0, 1.0) * notional)[:, :, None, None]
    trade_value = factor * annuity * (moneyness * (normal_cdf - offset) + spread * normal_pdf)
    occupied = lax.broadcasted_iota(jnp.int32, (groups, slot_count), 1) < block_count[:, None]
    trade_value = jnp.where(occupied[:, :, None, None], trade_value, 0.0)
    return jnp.sum(trade_value, axis=1).reshape(groups, -1)


def price_all(fields, discounts, dates_count):
    block_rows = fields[0].shape[0]
    group_size = max(32, block_rows // 16)
    turns = block_rows // group_size

    def regroup(array):
        return array.reshape((turns, group_size) + array.shape[1:])

    def one_group(pieces):
        return price_blocks(
            pieces[0],
            pieces[1],
            pieces[2],
            pieces[3],
            pieces[4],
            pieces[5],
            pieces[6],
            discounts,
            dates_count,
        )

    totals = lax.map(one_group, tuple((regroup(field) for field in fields)))
    return totals.reshape(block_rows, -1)


def shards_by_sum(
    shocks, trade_kind, cash_start, cash_count, strike, normal_vol, notional, block_count, block_set
):
    dates_count = shocks.shape[1]
    own_states = evolve(shocks.reshape(2, dates_count, -1))
    gathered = lax.all_gather(own_states, "trade", axis=2, tiled=True)
    discounts = discount_table(gathered)
    discounts = discounts.reshape(GRID, -1)
    block_total = price_all(
        (trade_kind, cash_start, cash_count, strike, normal_vol, notional, block_count),
        discounts,
        dates_count,
    )
    set_index = lax.broadcasted_iota(jnp.int32, (SET_DEV * lax.axis_size("trade"), 1), 0)
    one_hot = (set_index == block_set[None, :]).astype(jnp.float32)
    netted = lax.psum_scatter(
        jnp.dot(one_hot, block_total, precision=HIGHEST, preferred_element_type=jnp.float32),
        "trade",
        scatter_dimension=0,
        tiled=True,
    )
    return jnp.maximum(netted, 0.0).reshape(SET_DEV, dates_count, -1)


SLOTS_TILE = 8
LANES = 128
FIELDS = 6
ROWS = (FIELDS + 1) * SLOTS_TILE
DATES = 2

TAIL = (
    -1.325748085975647,
    -1.8081499338150024,
    -0.4117443561553955,
    -0.0426594540476799,
    0.0026849275454878807,
    0.0004979888908565044,
    -0.00017640502483118325,
    2.543121991038788e-05,
    -1.9144790712743998e-06,
    6.075951120010359e-08,
)
TAIL_END = 10.0


def iota(shape, dimension):
    return lax.broadcasted_iota(jnp.int32, shape, dimension)


def pack(kind, start, count, strike, vol, notional, live, group, shocks, out):
    slot_count, blocks = start.shape
    half = LANES // 2
    low = iota((SLOTS_TILE, LANES), 1) < half
    row = iota((SLOTS_TILE, LANES), 0)
    first = start[...]
    kinds = kind[...]
    occupied = iota((slot_count, blocks), 0) < live[...]
    fields = (
        first.astype(jnp.float32),
        (first + count[...]).astype(jnp.float32),
        strike[...],
        vol[...],
        jnp.where(occupied, jnp.where(kinds == 2, 2.0, 1.0) * notional[...], 0.0),
        jnp.where(kinds == 1, 1.0, jnp.where(kinds == 2, 0.5, 0.0)),
    )
    sets = jnp.broadcast_to((group[...] % SET_DEV).astype(jnp.float32), (SLOTS_TILE, blocks))
    extra = jnp.zeros((SLOTS_TILE, LANES), jnp.float32)
    for factor in range(2):
        for date in range(DATES):
            value = jnp.broadcast_to(shocks[factor : factor + 1, date : date + 1], (SLOTS_TILE, LANES))
            extra = jnp.where(row == 1 + factor * DATES + date, value, extra)
    for pair in range(blocks // LANES):
        cut = slice(pair * LANES, (pair + 1) * LANES)
        for at, field in enumerate(fields):
            top, bottom = field[:SLOTS_TILE, cut], field[SLOTS_TILE:, cut]
            here = slice(at * SLOTS_TILE, (at + 1) * SLOTS_TILE)
            out[2 * pair, here, :] = jnp.where(low, top, pltpu.roll(bottom, half, 1))
            out[2 * pair + 1, here, :] = jnp.where(low, pltpu.roll(top, half, 1), bottom)
        own = sets[:, cut]
        turned = pltpu.roll(own, half, 1)
        here = slice(FIELDS * SLOTS_TILE, ROWS)
        out[2 * pair, here, :] = jnp.where(row == 0, jnp.where(low, own, turned), extra)
        out[2 * pair + 1, here, :] = jnp.where(row == 0, jnp.where(low, turned, own), extra)


def split(values):
    parts = []
    for _ in range(3):
        part = values.astype(jnp.bfloat16)
        parts.append(part)
        values = values - part.astype(jnp.float32)
    return parts


def tables(shocks):
    node = iota((1, GRID), 1).astype(jnp.float32) * YEAR_STEP
    states = evolve(shocks)
    discounts = []
    for date in range(DATES):
        valued = (date + 1) * YEAR_STEP
        horizon = node - valued
        front = -FLAT_RATE * horizon + 0.5 * (
            factor_variance(horizon) - factor_variance(node) + factor_variance(jnp.full((1, GRID), valued))
        )
        discounts.append(
            jnp.exp(
                front
                - loading(REVERT_FAST, horizon) * states[0, date]
                - loading(REVERT_SLOW, horizon) * states[1, date]
            )
        )
    both = jnp.concatenate(discounts, axis=0)
    mid = GRID // 4
    source, target = iota((GRID, GRID), 0), iota((GRID, GRID), 1)
    weights = jnp.where((source > mid) & (source <= target), YEAR_STEP, 0.0) - jnp.where(
        (source <= mid) & (source > target), YEAR_STEP, 0.0
    )
    weights = weights.astype(jnp.bfloat16)
    sums = sum(
        jnp.dot(part, weights, preferred_element_type=jnp.float32) for part in reversed(split(both))
    )
    return both, sums


def price(ref, out, discount, running, totals):
    sources = ref.shape[0]
    extra = FIELDS * SLOTS_TILE
    shocks = jnp.stack(
        [jnp.stack([ref[:, extra + 1 + factor * DATES + date, :] for date in range(DATES)]) for factor in range(2)]
    )
    discount[...], running[...] = tables(shocks)
    row = iota((SLOTS_TILE, LANES), 0)
    masks = [(row & bit) == 0 for bit in (1, 2, 4)]

    def one_source(source, carry):
        def field(at):
            return ref[source, at * SLOTS_TILE : (at + 1) * SLOTS_TILE, :]

        first, last = field(0), field(1)
        first_node, last_node = first.astype(jnp.int32), last.astype(jnp.int32)
        strike, vol, size, offset = field(2), field(3), field(4), field(5)
        tilt = 0.5 - offset
        for date in range(DATES):
            spread = vol * jnp.sqrt(first * YEAR_STEP - (date + 1) * YEAR_STEP)
            inverse = 1.0 / spread
            scale = size * spread
            values = []
            for path in range(SLOTS_TILE):
                at = date * SLOTS_TILE + path
                curve = jnp.broadcast_to(discount[at : at + 1, :], (SLOTS_TILE, LANES))
                sums = jnp.broadcast_to(running[at : at + 1, :], (SLOTS_TILE, LANES))
                float_leg = jnp.take_along_axis(curve, first_node, axis=1) - jnp.take_along_axis(
                    curve, last_node, axis=1
                )
                annuity = jnp.take_along_axis(sums, last_node, axis=1) - jnp.take_along_axis(
                    sums, first_node, axis=1
                )
                standard = (float_leg / annuity - strike) * inverse
                size_of = jnp.abs(standard)
                capped = jnp.minimum(size_of, TAIL_END)
                power = jnp.full_like(capped, TAIL[-1])
                for term in TAIL[-2::-1]:
                    power = power * capped + term
                tail = jnp.exp2(power)
                values.append(scale * annuity * (0.5 * size_of + tilt * standard + tail))
            for bit, mask in zip((1, 2, 4), masks):
                values = [
                    jnp.where(mask, a, b) + pltpu.roll(jnp.where(mask, b, a), bit, 0)
                    for a, b in zip(values[::2], values[1::2])
                ]
            totals[source, date * SLOTS_TILE : (date + 1) * SLOTS_TILE, :] = values[0]
        return carry

    lax.fori_loop(0, sources, one_source, 0)
    set_index = iota((SET_DEV, LANES), 0).astype(jnp.float32)
    netted = jnp.zeros((DATES * SLOTS_TILE, SET_DEV), jnp.float32)
    for source in range(sources):
        one_hot = (set_index == ref[source, extra : extra + 1, :]).astype(jnp.float32)
        netted = netted + lax.dot_general(
            totals[source],
            one_hot,
            (((1,), (1,)), ((), ())),
            precision=HIGHEST,
            preferred_element_type=jnp.float32,
        )
    out[...] = jnp.maximum(netted, 0.0)


def shards_by_trade(
    shocks, trade_kind, cash_start, cash_count, strike, normal_vol, notional, block_count, block_set
):
    dates_count = shocks.shape[1]
    owners = lax.axis_size("trade")
    message = pl.pallas_call(
        pack, out_shape=jax.ShapeDtypeStruct((owners, ROWS, LANES), jnp.float32), name="pack"
    )(
        trade_kind.T,
        cash_start.T,
        cash_count.T,
        strike.T,
        normal_vol.T,
        notional.T,
        block_count.reshape(1, -1),
        block_set.reshape(1, -1),
        shocks.reshape(2, dates_count),
    )
    received = lax.all_to_all(message, "trade", 0, 0, tiled=True)
    netted = pl.pallas_call(
        price,
        out_shape=jax.ShapeDtypeStruct((dates_count * SLOTS_TILE, SET_DEV), jnp.float32),
        scratch_shapes=[
            pltpu.VMEM((dates_count * SLOTS_TILE, GRID), jnp.float32),
            pltpu.VMEM((dates_count * SLOTS_TILE, GRID), jnp.float32),
            pltpu.VMEM((owners, dates_count * SLOTS_TILE, LANES), jnp.float32),
        ],
        name="price",
    )(received)
    return netted.reshape(dates_count, SLOTS_TILE, SET_DEV).transpose(2, 0, 1)


def shards(shocks, trade_kind, *others):
    blocks, slot_count = trade_kind.shape
    by_trade = (
        lax.axis_size("trade") == SLOTS_TILE
        and shocks.shape == (2, DATES, 1, 1)
        and slot_count == 2 * SLOTS_TILE
        and blocks == SLOTS_TILE * LANES // 2
    )
    return (shards_by_trade if by_trade else shards_by_sum)(shocks, trade_kind, *others)


def solution(mesh):
    placed = (
        P("book", None, "path", "trade"),
        P(("book", "trade"), None),
        P(("book", "trade"), None),
        P(("book", "trade"), None),
        P(("book", "trade"), None),
        P(("book", "trade"), None),
        P(("book", "trade"), None),
        P(("book", "trade")),
        P(("book", "trade")),
    )
    return jax.shard_map(
        shards,
        mesh=mesh,
        in_specs=placed,
        out_specs=P(("book", "trade"), None, "path"),
        check_vma=False,
    )
```

```python
import math

import jax
import jax.numpy as jnp
from jax import lax
from jax.experimental import pallas as pl
from jax.experimental.pallas import tpu as pltpu
from jax.sharding import PartitionSpec as P

GRID = 128
SET_DEV = 32


YEAR_STEP = 0.25
FLAT_RATE = 0.03
REVERT_FAST = 0.5
REVERT_SLOW = 0.04
VOL_FAST = 0.012
VOL_SLOW = 0.009
FACTOR_CORR = -0.6
HIGHEST = lax.Precision.HIGHEST


def loading(reversion, horizon):
    return (1.0 - jnp.exp(-reversion * horizon)) / reversion


def one_variance(reversion, volatility, horizon):
    return (
        volatility**2
        / reversion**2
        * (
            horizon
            + 2.0 / reversion * jnp.exp(-reversion * horizon)
            - 0.5 / reversion * jnp.exp(-2.0 * reversion * horizon)
            - 1.5 / reversion
        )
    )


def factor_variance(horizon):
    fast_part = one_variance(REVERT_FAST, VOL_FAST, horizon)
    slow_part = one_variance(REVERT_SLOW, VOL_SLOW, horizon)
    both_rates = REVERT_FAST + REVERT_SLOW
    cross_part = (
        2.0
        * FACTOR_CORR
        * VOL_FAST
        * VOL_SLOW
        / (REVERT_FAST * REVERT_SLOW)
        * (
            horizon
            + (jnp.exp(-REVERT_FAST * horizon) - 1.0) / REVERT_FAST
            + (jnp.exp(-REVERT_SLOW * horizon) - 1.0) / REVERT_SLOW
            - (jnp.exp(-both_rates * horizon) - 1.0) / both_rates
        )
    )
    return fast_part + slow_part + cross_part


def evolve(path_shocks):
    fast_keep = math.exp(-REVERT_FAST * YEAR_STEP)
    slow_keep = math.exp(-REVERT_SLOW * YEAR_STEP)
    fast_scale = VOL_FAST * math.sqrt(
        (1.0 - math.exp(-2.0 * REVERT_FAST * YEAR_STEP)) / (2.0 * REVERT_FAST)
    )
    slow_scale = VOL_SLOW * math.sqrt(
        (1.0 - math.exp(-2.0 * REVERT_SLOW * YEAR_STEP)) / (2.0 * REVERT_SLOW)
    )
    mixing = math.sqrt(1.0 - FACTOR_CORR**2)
    fast_state = jnp.zeros(path_shocks.shape[2:], jnp.float32)
    slow_state = jnp.zeros(path_shocks.shape[2:], jnp.float32)
    fast_path = []
    slow_path = []
    for period in range(path_shocks.shape[1]):
        fast_state = fast_state * fast_keep + fast_scale * path_shocks[0, period]
        slow_state = slow_state * slow_keep + slow_scale * (
            FACTOR_CORR * path_shocks[0, period] + mixing * path_shocks[1, period]
        )
        fast_path.append(fast_state)
        slow_path.append(slow_state)
    return jnp.stack([jnp.stack(fast_path), jnp.stack(slow_path)])


def discount_table(states):
    dates_count = states.shape[1]
    maturity = lax.broadcasted_iota(jnp.int32, (GRID, 1, 1), 0).astype(jnp.float32) * YEAR_STEP
    valued = (lax.broadcasted_iota(jnp.int32, (1, dates_count, 1), 1) + 1).astype(
        jnp.float32
    ) * YEAR_STEP
    horizon = maturity - valued
    log_front = -FLAT_RATE * horizon + 0.5 * (
        factor_variance(horizon) - factor_variance(maturity) + factor_variance(valued)
    )
    return jnp.exp(
        log_front
        - loading(REVERT_FAST, horizon) * states[0][None]
        - loading(REVERT_SLOW, horizon) * states[1][None]
    )


def price_blocks(
    trade_kind,
    cash_start,
    cash_count,
    strike,
    normal_vol,
    notional,
    block_count,
    discounts,
    dates_count,
):
    groups, slot_count = cash_start.shape
    cash_nodes = lax.broadcasted_iota(jnp.int32, (1, 1, GRID), 2)
    first_node = cash_start[:, :, None]
    last_node = (cash_start + cash_count)[:, :, None]
    accrual = jnp.where(
        (cash_nodes > first_node) & (cash_nodes <= last_node), YEAR_STEP, 0.0
    ).astype(jnp.float32)
    endpoints = (
        jnp.where(cash_nodes == first_node, 1.0, 0.0) - jnp.where(cash_nodes == last_node, 1.0, 0.0)
    ).astype(jnp.float32)
    weights = jnp.concatenate([accrual, endpoints], axis=0).reshape(2 * groups * slot_count, GRID)
    products = jnp.dot(weights, discounts, precision=HIGHEST, preferred_element_type=jnp.float32)
    products = products.reshape(2, groups, slot_count, dates_count, -1)
    annuity = products[0]
    float_leg = products[1]
    swap_rate = float_leg / annuity
    valued = (lax.broadcasted_iota(jnp.int32, (1, 1, dates_count, 1), 2) + 1).astype(
        jnp.float32
    ) * YEAR_STEP
    expiry = cash_start.astype(jnp.float32)[:, :, None, None] * YEAR_STEP
    spread = normal_vol[:, :, None, None] * jnp.sqrt(expiry - valued)
    moneyness = swap_rate - strike[:, :, None, None]
    standard = moneyness / spread
    normal_cdf = 0.5 * (1.0 + jax.scipy.special.erf(standard * (1.0 / math.sqrt(2.0))))
    normal_pdf = jnp.exp(-0.5 * standard * standard) * (1.0 / math.sqrt(2.0 * math.pi))
    offset = jnp.where(trade_kind == 1, 1.0, jnp.where(trade_kind == 2, 0.5, 0.0))[:, :, None, None]
    factor = (jnp.where(trade_kind == 2, 2.0, 1.0) * notional)[:, :, None, None]
    trade_value = factor * annuity * (moneyness * (normal_cdf - offset) + spread * normal_pdf)
    occupied = lax.broadcasted_iota(jnp.int32, (groups, slot_count), 1) < block_count[:, None]
    trade_value = jnp.where(occupied[:, :, None, None], trade_value, 0.0)
    return jnp.sum(trade_value, axis=1).reshape(groups, -1)


def price_all(fields, discounts, dates_count):
    block_rows = fields[0].shape[0]
    group_size = max(32, block_rows // 16)
    turns = block_rows // group_size

    def regroup(array):
        return array.reshape((turns, group_size) + array.shape[1:])

    def one_group(pieces):
        return price_blocks(
            pieces[0],
            pieces[1],
            pieces[2],
            pieces[3],
            pieces[4],
            pieces[5],
            pieces[6],
            discounts,
            dates_count,
        )

    totals = lax.map(one_group, tuple((regroup(field) for field in fields)))
    return totals.reshape(block_rows, -1)


def shards_by_sum(
    shocks, trade_kind, cash_start, cash_count, strike, normal_vol, notional, block_count, block_set
):
    dates_count = shocks.shape[1]
    own_states = evolve(shocks.reshape(2, dates_count, -1))
    gathered = lax.all_gather(own_states, "trade", axis=2, tiled=True)
    discounts = discount_table(gathered)
    discounts = discounts.reshape(GRID, -1)
    block_total = price_all(
        (trade_kind, cash_start, cash_count, strike, normal_vol, notional, block_count),
        discounts,
        dates_count,
    )
    set_index = lax.broadcasted_iota(jnp.int32, (SET_DEV * lax.axis_size("trade"), 1), 0)
    one_hot = (set_index == block_set[None, :]).astype(jnp.float32)
    netted = lax.psum_scatter(
        jnp.dot(one_hot, block_total, precision=HIGHEST, preferred_element_type=jnp.float32),
        "trade",
        scatter_dimension=0,
        tiled=True,
    )
    return jnp.maximum(netted, 0.0).reshape(SET_DEV, dates_count, -1)


SLOTS_TILE = 8
LANES = 128
FIELDS = 6
ROWS = (FIELDS + 1) * SLOTS_TILE
DATES = 2
VMEM_BYTES = 8 * 2**20

TAIL = (
    -1.325748085975647,
    -1.8081499338150024,
    -0.4117443561553955,
    -0.0426594540476799,
    0.0026849275454878807,
    0.0004979888908565044,
    -0.00017640502483118325,
    2.543121991038788e-05,
    -1.9144790712743998e-06,
    6.075951120010359e-08,
)
TAIL_END = 10.0


def iota(shape, dimension):
    return lax.broadcasted_iota(jnp.int32, shape, dimension)


def pack(*refs):
    count_of = len(refs) // 2 - 1
    sources, out, held, arrived = refs[:count_of], refs[count_of], refs[count_of + 1 : -1], refs[-1]
    copies = [
        pltpu.make_async_copy(source, target, arrived.at[at])
        for at, (source, target) in enumerate(zip(sources, held))
    ]
    for copy in copies:
        copy.start()
    for copy in copies:
        copy.wait()
    kind, start, count, strike, vol, notional, live, group, shocks = held
    slot_count, blocks = start.shape
    half = LANES // 2
    low = iota((SLOTS_TILE, LANES), 1) < half
    row = iota((SLOTS_TILE, LANES), 0)
    first = start[...]
    kinds = kind[...]
    occupied = iota((slot_count, blocks), 0) < live[...]
    fields = (
        first.astype(jnp.float32),
        (first + count[...]).astype(jnp.float32),
        strike[...],
        vol[...],
        jnp.where(occupied, jnp.where(kinds == 2, 2.0, 1.0) * notional[...], 0.0),
        jnp.where(kinds == 1, 1.0, jnp.where(kinds == 2, 0.5, 0.0)),
    )
    sets = jnp.broadcast_to((group[...] % SET_DEV).astype(jnp.float32), (SLOTS_TILE, blocks))
    extra = jnp.zeros((SLOTS_TILE, LANES), jnp.float32)
    for factor in range(2):
        for date in range(DATES):
            value = jnp.broadcast_to(shocks[factor : factor + 1, date : date + 1], (SLOTS_TILE, LANES))
            extra = jnp.where(row == 1 + factor * DATES + date, value, extra)
    for pair in range(blocks // LANES):
        cut = slice(pair * LANES, (pair + 1) * LANES)
        for at, field in enumerate(fields):
            top, bottom = field[:SLOTS_TILE, cut], field[SLOTS_TILE:, cut]
            here = slice(at * SLOTS_TILE, (at + 1) * SLOTS_TILE)
            out[2 * pair, here, :] = jnp.where(low, top, pltpu.roll(bottom, half, 1))
            out[2 * pair + 1, here, :] = jnp.where(low, pltpu.roll(top, half, 1), bottom)
        own = sets[:, cut]
        turned = pltpu.roll(own, half, 1)
        here = slice(FIELDS * SLOTS_TILE, ROWS)
        out[2 * pair, here, :] = jnp.where(row == 0, jnp.where(low, own, turned), extra)
        out[2 * pair + 1, here, :] = jnp.where(row == 0, jnp.where(low, turned, own), extra)


def split(values):
    parts = []
    for _ in range(3):
        part = values.astype(jnp.bfloat16)
        parts.append(part)
        values = values - part.astype(jnp.float32)
    return parts


def tables(shocks):
    node = iota((1, GRID), 1).astype(jnp.float32) * YEAR_STEP
    states = evolve(shocks)
    discounts = []
    for date in range(DATES):
        valued = (date + 1) * YEAR_STEP
        horizon = node - valued
        front = -FLAT_RATE * horizon + 0.5 * (
            factor_variance(horizon) - factor_variance(node) + factor_variance(jnp.full((1, GRID), valued))
        )
        discounts.append(
            jnp.exp(
                front
                - loading(REVERT_FAST, horizon) * states[0, date]
                - loading(REVERT_SLOW, horizon) * states[1, date]
            )
        )
    both = jnp.concatenate(discounts, axis=0)
    mid = GRID // 4
    source, target = iota((GRID, GRID), 0), iota((GRID, GRID), 1)
    weights = jnp.where((source > mid) & (source <= target), YEAR_STEP, 0.0) - jnp.where(
        (source <= mid) & (source > target), YEAR_STEP, 0.0
    )
    weights = weights.astype(jnp.bfloat16)
    sums = sum(
        jnp.dot(part, weights, preferred_element_type=jnp.float32) for part in reversed(split(both))
    )
    return both, sums


def price(ref, out, discount, running, totals):
    sources = ref.shape[0]
    extra = FIELDS * SLOTS_TILE
    shocks = jnp.stack(
        [jnp.stack([ref[:, extra + 1 + factor * DATES + date, :] for date in range(DATES)]) for factor in range(2)]
    )
    discount[...], running[...] = tables(shocks)
    row = iota((SLOTS_TILE, LANES), 0)
    masks = [(row & bit) == 0 for bit in (1, 2, 4)]

    def one_source(source, carry):
        def field(at):
            return ref[source, at * SLOTS_TILE : (at + 1) * SLOTS_TILE, :]

        first, last = field(0), field(1)
        first_node, last_node = first.astype(jnp.int32), last.astype(jnp.int32)
        strike, vol, size, offset = field(2), field(3), field(4), field(5)
        tilt = 0.5 - offset
        for date in range(DATES):
            spread = vol * jnp.sqrt(first * YEAR_STEP - (date + 1) * YEAR_STEP)
            inverse = 1.0 / spread
            scale = size * spread
            values = []
            for path in range(SLOTS_TILE):
                at = date * SLOTS_TILE + path
                curve = jnp.broadcast_to(discount[at : at + 1, :], (SLOTS_TILE, LANES))
                sums = jnp.broadcast_to(running[at : at + 1, :], (SLOTS_TILE, LANES))
                float_leg = jnp.take_along_axis(curve, first_node, axis=1) - jnp.take_along_axis(
                    curve, last_node, axis=1
                )
                annuity = jnp.take_along_axis(sums, last_node, axis=1) - jnp.take_along_axis(
                    sums, first_node, axis=1
                )
                standard = (float_leg / annuity - strike) * inverse
                size_of = jnp.abs(standard)
                capped = jnp.minimum(size_of, TAIL_END)
                power = jnp.full_like(capped, TAIL[-1])
                for term in TAIL[-2::-1]:
                    power = power * capped + term
                tail = jnp.exp2(power)
                values.append(scale * annuity * (0.5 * size_of + tilt * standard + tail))
            for bit, mask in zip((1, 2, 4), masks):
                values = [
                    jnp.where(mask, a, b) + pltpu.roll(jnp.where(mask, b, a), bit, 0)
                    for a, b in zip(values[::2], values[1::2])
                ]
            totals[source, date * SLOTS_TILE : (date + 1) * SLOTS_TILE, :] = values[0]
        return carry

    for source in range(sources):
        one_source(source, 0)
    set_index = iota((SET_DEV, LANES), 0).astype(jnp.float32)
    netted = jnp.zeros((DATES * SLOTS_TILE, SET_DEV), jnp.float32)
    for source in range(sources):
        one_hot = (set_index == ref[source, extra : extra + 1, :]).astype(jnp.float32)
        netted = netted + lax.dot_general(
            totals[source],
            one_hot,
            (((1,), (1,)), ((), ())),
            precision=HIGHEST,
            preferred_element_type=jnp.float32,
        )
    out[...] = jnp.maximum(netted, 0.0)


def shards_by_trade(
    shocks, trade_kind, cash_start, cash_count, strike, normal_vol, notional, block_count, block_set
):
    dates_count = shocks.shape[1]
    owners = lax.axis_size("trade")
    fields = (
        trade_kind.T,
        cash_start.T,
        cash_count.T,
        strike.T,
        normal_vol.T,
        notional.T,
        block_count.reshape(1, -1),
        block_set.reshape(1, -1),
        shocks.reshape(2, dates_count),
    )
    message = pl.pallas_call(
        pack,
        out_shape=jax.ShapeDtypeStruct((owners, ROWS, LANES), jnp.float32),
        in_specs=[pl.BlockSpec(memory_space=pltpu.HBM)] * len(fields),
        scratch_shapes=[pltpu.VMEM(field.shape, field.dtype) for field in fields]
        + [pltpu.SemaphoreType.DMA((len(fields),))],
        compiler_params=pltpu.CompilerParams(vmem_limit_bytes=VMEM_BYTES),
        name="pack",
    )(*(pltpu.with_memory_space_constraint(field, pltpu.HBM) for field in fields))
    received = lax.all_to_all(message, "trade", 0, 0, tiled=True)
    netted = pl.pallas_call(
        price,
        out_shape=jax.ShapeDtypeStruct((dates_count * SLOTS_TILE, SET_DEV), jnp.float32),
        scratch_shapes=[
            pltpu.VMEM((dates_count * SLOTS_TILE, GRID), jnp.float32),
            pltpu.VMEM((dates_count * SLOTS_TILE, GRID), jnp.float32),
            pltpu.VMEM((owners, dates_count * SLOTS_TILE, LANES), jnp.float32),
        ],
        name="price",
        compiler_params=pltpu.CompilerParams(vmem_limit_bytes=VMEM_BYTES),
    )(received)
    return netted.reshape(dates_count, SLOTS_TILE, SET_DEV).transpose(2, 0, 1)


def shards(shocks, trade_kind, *others):
    blocks, slot_count = trade_kind.shape
    by_trade = (
        lax.axis_size("trade") == SLOTS_TILE
        and shocks.shape == (2, DATES, 1, 1)
        and slot_count == 2 * SLOTS_TILE
        and blocks == SLOTS_TILE * LANES // 2
    )
    return (shards_by_trade if by_trade else shards_by_sum)(shocks, trade_kind, *others)


def solution(mesh):
    placed = (
        P("book", None, "path", "trade"),
        P(("book", "trade"), None),
        P(("book", "trade"), None),
        P(("book", "trade"), None),
        P(("book", "trade"), None),
        P(("book", "trade"), None),
        P(("book", "trade"), None),
        P(("book", "trade")),
        P(("book", "trade")),
    )
    return jax.shard_map(
        shards,
        mesh=mesh,
        in_specs=placed,
        out_specs=P(("book", "trade"), None, "path"),
        check_vma=False,
    )
```

```python
import math

import jax
import jax.numpy as jnp
from jax import lax
from jax.experimental import pallas as pl
from jax.experimental.pallas import tpu as pltpu
from jax.sharding import PartitionSpec as P

GRID = 128
SET_DEV = 32


YEAR_STEP = 0.25
FLAT_RATE = 0.03
REVERT_FAST = 0.5
REVERT_SLOW = 0.04
VOL_FAST = 0.012
VOL_SLOW = 0.009
FACTOR_CORR = -0.6
HIGHEST = lax.Precision.HIGHEST


def loading(reversion, horizon):
    return (1.0 - jnp.exp(-reversion * horizon)) / reversion


def one_variance(reversion, volatility, horizon):
    return (
        volatility**2
        / reversion**2
        * (
            horizon
            + 2.0 / reversion * jnp.exp(-reversion * horizon)
            - 0.5 / reversion * jnp.exp(-2.0 * reversion * horizon)
            - 1.5 / reversion
        )
    )


def factor_variance(horizon):
    fast_part = one_variance(REVERT_FAST, VOL_FAST, horizon)
    slow_part = one_variance(REVERT_SLOW, VOL_SLOW, horizon)
    both_rates = REVERT_FAST + REVERT_SLOW
    cross_part = (
        2.0
        * FACTOR_CORR
        * VOL_FAST
        * VOL_SLOW
        / (REVERT_FAST * REVERT_SLOW)
        * (
            horizon
            + (jnp.exp(-REVERT_FAST * horizon) - 1.0) / REVERT_FAST
            + (jnp.exp(-REVERT_SLOW * horizon) - 1.0) / REVERT_SLOW
            - (jnp.exp(-both_rates * horizon) - 1.0) / both_rates
        )
    )
    return fast_part + slow_part + cross_part


def evolve(path_shocks):
    fast_keep = math.exp(-REVERT_FAST * YEAR_STEP)
    slow_keep = math.exp(-REVERT_SLOW * YEAR_STEP)
    fast_scale = VOL_FAST * math.sqrt(
        (1.0 - math.exp(-2.0 * REVERT_FAST * YEAR_STEP)) / (2.0 * REVERT_FAST)
    )
    slow_scale = VOL_SLOW * math.sqrt(
        (1.0 - math.exp(-2.0 * REVERT_SLOW * YEAR_STEP)) / (2.0 * REVERT_SLOW)
    )
    mixing = math.sqrt(1.0 - FACTOR_CORR**2)
    fast_state = jnp.zeros(path_shocks.shape[2:], jnp.float32)
    slow_state = jnp.zeros(path_shocks.shape[2:], jnp.float32)
    fast_path = []
    slow_path = []
    for period in range(path_shocks.shape[1]):
        fast_state = fast_state * fast_keep + fast_scale * path_shocks[0, period]
        slow_state = slow_state * slow_keep + slow_scale * (
            FACTOR_CORR * path_shocks[0, period] + mixing * path_shocks[1, period]
        )
        fast_path.append(fast_state)
        slow_path.append(slow_state)
    return jnp.stack([jnp.stack(fast_path), jnp.stack(slow_path)])


def discount_table(states):
    dates_count = states.shape[1]
    maturity = lax.broadcasted_iota(jnp.int32, (GRID, 1, 1), 0).astype(jnp.float32) * YEAR_STEP
    valued = (lax.broadcasted_iota(jnp.int32, (1, dates_count, 1), 1) + 1).astype(
        jnp.float32
    ) * YEAR_STEP
    horizon = maturity - valued
    log_front = -FLAT_RATE * horizon + 0.5 * (
        factor_variance(horizon) - factor_variance(maturity) + factor_variance(valued)
    )
    return jnp.exp(
        log_front
        - loading(REVERT_FAST, horizon) * states[0][None]
        - loading(REVERT_SLOW, horizon) * states[1][None]
    )


def price_blocks(
    trade_kind,
    cash_start,
    cash_count,
    strike,
    normal_vol,
    notional,
    block_count,
    discounts,
    dates_count,
):
    groups, slot_count = cash_start.shape
    cash_nodes = lax.broadcasted_iota(jnp.int32, (1, 1, GRID), 2)
    first_node = cash_start[:, :, None]
    last_node = (cash_start + cash_count)[:, :, None]
    accrual = jnp.where(
        (cash_nodes > first_node) & (cash_nodes <= last_node), YEAR_STEP, 0.0
    ).astype(jnp.float32)
    endpoints = (
        jnp.where(cash_nodes == first_node, 1.0, 0.0) - jnp.where(cash_nodes == last_node, 1.0, 0.0)
    ).astype(jnp.float32)
    weights = jnp.concatenate([accrual, endpoints], axis=0).reshape(2 * groups * slot_count, GRID)
    products = jnp.dot(weights, discounts, precision=HIGHEST, preferred_element_type=jnp.float32)
    products = products.reshape(2, groups, slot_count, dates_count, -1)
    annuity = products[0]
    float_leg = products[1]
    swap_rate = float_leg / annuity
    valued = (lax.broadcasted_iota(jnp.int32, (1, 1, dates_count, 1), 2) + 1).astype(
        jnp.float32
    ) * YEAR_STEP
    expiry = cash_start.astype(jnp.float32)[:, :, None, None] * YEAR_STEP
    spread = normal_vol[:, :, None, None] * jnp.sqrt(expiry - valued)
    moneyness = swap_rate - strike[:, :, None, None]
    standard = moneyness / spread
    normal_cdf = 0.5 * (1.0 + jax.scipy.special.erf(standard * (1.0 / math.sqrt(2.0))))
    normal_pdf = jnp.exp(-0.5 * standard * standard) * (1.0 / math.sqrt(2.0 * math.pi))
    offset = jnp.where(trade_kind == 1, 1.0, jnp.where(trade_kind == 2, 0.5, 0.0))[:, :, None, None]
    factor = (jnp.where(trade_kind == 2, 2.0, 1.0) * notional)[:, :, None, None]
    trade_value = factor * annuity * (moneyness * (normal_cdf - offset) + spread * normal_pdf)
    occupied = lax.broadcasted_iota(jnp.int32, (groups, slot_count), 1) < block_count[:, None]
    trade_value = jnp.where(occupied[:, :, None, None], trade_value, 0.0)
    return jnp.sum(trade_value, axis=1).reshape(groups, -1)


def price_all(fields, discounts, dates_count):
    block_rows = fields[0].shape[0]
    group_size = max(32, block_rows // 16)
    turns = block_rows // group_size

    def regroup(array):
        return array.reshape((turns, group_size) + array.shape[1:])

    def one_group(pieces):
        return price_blocks(
            pieces[0],
            pieces[1],
            pieces[2],
            pieces[3],
            pieces[4],
            pieces[5],
            pieces[6],
            discounts,
            dates_count,
        )

    totals = lax.map(one_group, tuple((regroup(field) for field in fields)))
    return totals.reshape(block_rows, -1)


def shards_by_sum(
    shocks, trade_kind, cash_start, cash_count, strike, normal_vol, notional, block_count, block_set
):
    dates_count = shocks.shape[1]
    own_states = evolve(shocks.reshape(2, dates_count, -1))
    gathered = lax.all_gather(own_states, "trade", axis=2, tiled=True)
    discounts = discount_table(gathered)
    discounts = discounts.reshape(GRID, -1)
    block_total = price_all(
        (trade_kind, cash_start, cash_count, strike, normal_vol, notional, block_count),
        discounts,
        dates_count,
    )
    set_index = lax.broadcasted_iota(jnp.int32, (SET_DEV * lax.axis_size("trade"), 1), 0)
    one_hot = (set_index == block_set[None, :]).astype(jnp.float32)
    netted = lax.psum_scatter(
        jnp.dot(one_hot, block_total, precision=HIGHEST, preferred_element_type=jnp.float32),
        "trade",
        scatter_dimension=0,
        tiled=True,
    )
    return jnp.maximum(netted, 0.0).reshape(SET_DEV, dates_count, -1)


SLOTS_TILE = 8
LANES = 128
FIELDS = 6
ROWS = (FIELDS + 1) * SLOTS_TILE
INPUTS = range(9)
NEAR = 1
FAR = ((3, 6), (2, 5), (4, 7))
DATES = 2
VMEM_BYTES = 8 * 2**20

TAIL = (
    -1.325748085975647,
    -1.8081518411636353,
    -0.41172587871551514,
    -0.042724475264549255,
    0.0027914412785321474,
    0.00040712140616960824,
    -0.00013435240543913096,
    1.5000393432273995e-05,
    -6.33199476851587e-07,
)


def iota(shape, dimension):
    return lax.broadcasted_iota(jnp.int32, shape, dimension)


def offsets(core):
    return [NEAR] + [jnp.where(core == 0, first, second) for first, second in FAR]


def pack(*refs):
    count_of = len(INPUTS)
    sources, outs = refs[:count_of], refs[count_of : count_of + 2 + len(FAR)]
    grid = refs[count_of + 2 + len(FAR)]
    held, arrived = refs[count_of + 3 + len(FAR) : -1], refs[-1]
    copies = [
        pltpu.make_async_copy(source, target, arrived.at[at])
        for at, (source, target) in enumerate(zip(sources, held))
    ]
    for copy in copies:
        copy.start()
    for at, rows in enumerate(curve_rows()):
        grid[at] = rows
    me, core = lax.axis_index("trade"), lax.axis_index("path")
    half = LANES // 2
    low = iota((SLOTS_TILE, LANES), 1) < half
    row, lane = iota((SLOTS_TILE, LANES), 0), iota((SLOTS_TILE, LANES), 1)
    for copy in copies:
        copy.wait()
    kind, start, count, strike, vol, notional, live, group, shocks = held
    own_shocks = jnp.zeros((SLOTS_TILE, LANES), jnp.float32)
    for factor in range(2):
        for date in range(DATES):
            value = jnp.broadcast_to(shocks[factor : factor + 1, date : date + 1], (SLOTS_TILE, LANES))
            own_shocks = jnp.where(lane == factor * DATES + date, value, own_shocks)
    for out, offset in zip(outs, [0] + offsets(core)):
        owner = me ^ offset
        cut = pl.ds(pl.multiple_of(owner // 2 * LANES, LANES), LANES)
        odd = owner % 2

        def both(low_half, high_half):
            return jnp.where(
                low, pltpu.roll(low_half, half * odd, 1), pltpu.roll(high_half, half * (1 - odd), 1)
            )

        def field(ref):
            return both(ref[:SLOTS_TILE, cut], ref[SLOTS_TILE:, cut])

        lives = jnp.broadcast_to(live[:, cut], (SLOTS_TILE, LANES))
        sets = jnp.broadcast_to(group[:, cut], (SLOTS_TILE, LANES))
        slot = row + jnp.where(low, 0, SLOTS_TILE)
        first, kinds = field(start), field(kind)
        size = jnp.where(kinds == 2, 2.0, 1.0) * field(notional)
        tiles = (
            first.astype(jnp.float32),
            (first + field(count)).astype(jnp.float32),
            field(strike),
            field(vol),
            jnp.where(slot < both(lives, lives), size, 0.0),
            jnp.where(kinds == 1, 1.0, jnp.where(kinds == 2, 0.5, 0.0)),
            jnp.where(row == 0, (both(sets, sets) - owner * SET_DEV).astype(jnp.float32), own_shocks),
        )
        for at, tile in enumerate(tiles):
            out[at * SLOTS_TILE : (at + 1) * SLOTS_TILE, :] = tile


def add_shocks(shocks, *refs):
    core = lax.axis_index("path")
    lane = iota((1, LANES), 1)
    line = jnp.zeros((1, LANES), jnp.float32)
    for factor in range(2):
        for date in range(DATES):
            value = jnp.broadcast_to(shocks[factor : factor + 1, date : date + 1], (1, LANES))
            line = jnp.where(lane == factor * DATES + date, value, line)
    for ref in refs[len(FAR) :]:
        ref[pl.ds(FIELDS * SLOTS_TILE + 2 - core, 1), :] = line


def split(values, count):
    parts = []
    for _ in range(count):
        part = values.astype(jnp.bfloat16)
        parts.append(part)
        values = values - part.astype(jnp.float32)
    return jnp.concatenate(parts, axis=0)


def add_parts(product, count):
    rows = product.shape[0] // count
    total = product[(count - 1) * rows :]
    for part in range(count - 2, -1, -1):
        total = total + product[part * rows : (part + 1) * rows]
    return total


def curve_rows():
    node = iota((SLOTS_TILE, GRID), 1).astype(jnp.float32) * YEAR_STEP
    row = iota((SLOTS_TILE, GRID), 0)
    valued = jnp.where(row < DATES + 1, row, 1).astype(jnp.float32) * YEAR_STEP
    horizon = node - valued
    front = -FLAT_RATE * horizon + 0.5 * (
        factor_variance(horizon) - factor_variance(node) + factor_variance(valued)
    )
    return front, loading(REVERT_FAST, horizon), loading(REVERT_SLOW, horizon)


def tables(shocks, grid):
    states = evolve(shocks)
    discounts = []
    for date in range(DATES):
        front, fast, slow = (grid[at, date + 1 : date + 2, :] for at in range(3))
        discounts.append(jnp.exp(front - fast * states[0, date] - slow * states[1, date]))
    both = jnp.concatenate(discounts, axis=0)
    mid = GRID // 4
    source, target = iota((GRID, GRID), 0), iota((GRID, GRID), 1)
    weights = jnp.where((source > mid) & (source <= target), YEAR_STEP, 0.0) - jnp.where(
        (source <= mid) & (source > target), YEAR_STEP, 0.0
    )
    sums = jnp.dot(split(both, 3), weights.astype(jnp.bfloat16), preferred_element_type=jnp.float32)
    return both, add_parts(sums, 3)


def price_source(ref, discount, running, masks):
    def field(at):
        return ref[at * SLOTS_TILE : (at + 1) * SLOTS_TILE, :]

    def look_up(table, at, index):
        row = jnp.broadcast_to(table[at : at + 1, :], (SLOTS_TILE, LANES))
        return jnp.take_along_axis(row, index, axis=1, mode="promise_in_bounds")

    first, last = field(0), field(1)
    first_node, last_node = first.astype(jnp.int32), last.astype(jnp.int32)
    strike, vol, size, offset = field(2), field(3), field(4), field(5)
    tilt = 0.5 - offset
    totals = []
    for date in range(DATES):
        spread = vol * jnp.sqrt(first * YEAR_STEP - (date + 1) * YEAR_STEP)
        inverse = 1.0 / spread
        scale = size * spread
        hurdle = strike * inverse
        rows = range(date * SLOTS_TILE, (date + 1) * SLOTS_TILE)
        starts = [(look_up(discount, at, first_node), look_up(running, at, first_node)) for at in rows]
        ends = [(look_up(discount, at, last_node), look_up(running, at, last_node)) for at in rows]
        values = []
        for (curve_start, sum_start), (curve_end, sum_end) in zip(starts, ends):
            float_leg, annuity = curve_start - curve_end, sum_end - sum_start
            standard = float_leg * pl.reciprocal(annuity) * inverse - hurdle
            size_of = jnp.abs(standard)
            power = jnp.full_like(size_of, TAIL[-1])
            for term in TAIL[-2::-1]:
                power = power * size_of + term
            values.append(scale * annuity * (0.5 * size_of + tilt * standard + jnp.exp2(power)))
        for bit, mask in zip((1, 2, 4), masks):
            values = [
                jnp.where(mask, a, b) + pltpu.roll(jnp.where(mask, b, a), bit, 0)
                for a, b in zip(values[::2], values[1::2])
            ]
        totals.append(values[0])
    return jnp.concatenate(totals, axis=0)


def price(*refs):
    refs, (grid, out, discount, running) = refs[:-4], refs[-4:]
    extra = FIELDS * SLOTS_TILE
    me, core = lax.axis_index("trade"), lax.axis_index("path")
    row = iota((SLOTS_TILE, LANES), 0)
    lines = jnp.zeros((SLOTS_TILE, LANES), jnp.float32)
    for ref, offset in zip(refs, [0] + offsets(core) + offsets(1 - core)[1:]):
        line = jnp.broadcast_to(ref[pl.ds(extra + 1 + core, 1), :], (SLOTS_TILE, LANES))
        lines = jnp.where(row == (me ^ offset), line, lines)
    shocks = jnp.stack(
        [
            jnp.stack(
                [
                    jnp.broadcast_to(lines[:, at : at + 1], (SLOTS_TILE, LANES))
                    for at in range(factor * DATES, (factor + 1) * DATES)
                ]
            )
            for factor in range(2)
        ]
    )
    discount[...], running[...] = tables(shocks, grid)
    masks = [(row & bit) == 0 for bit in (1, 2, 4)]
    set_index = iota((SET_DEV, LANES), 0).astype(jnp.float32)
    one_hot = jnp.concatenate(
        [(set_index == ref[extra : extra + 1, :]).astype(jnp.bfloat16) for ref in refs], axis=1
    )
    totals = jnp.concatenate([price_source(ref, discount, running, masks) for ref in refs], axis=1)
    netted = lax.dot_general(
        split(totals, 3), one_hot, (((1,), (1,)), ((), ())), preferred_element_type=jnp.float32
    )
    out[...] = jnp.maximum(add_parts(netted, 3), 0.0)


def shards_by_trade(
    shocks, trade_kind, cash_start, cash_count, strike, normal_vol, notional, block_count, block_set
):
    dates_count = shocks.shape[1]
    own_shocks = shocks.reshape(2, dates_count)
    swap = [(0, 1), (1, 0)]
    other_shocks = lax.ppermute(own_shocks, "path", swap)
    fields = (
        trade_kind.T,
        cash_start.T,
        cash_count.T,
        strike.T,
        normal_vol.T,
        notional.T,
        block_count.reshape(1, -1),
        block_set.reshape(1, -1),
        own_shocks,
    )
    message = jax.ShapeDtypeStruct((ROWS, LANES), jnp.float32)
    limit = pltpu.CompilerParams(vmem_limit_bytes=VMEM_BYTES)
    own, near, *far, grid = pl.pallas_call(
        pack,
        out_shape=[message] * (2 + len(FAR)) + [jax.ShapeDtypeStruct((3, SLOTS_TILE, GRID), jnp.float32)],
        in_specs=[pl.BlockSpec(memory_space=pltpu.HBM)] * len(fields),
        scratch_shapes=[pltpu.VMEM(field.shape, field.dtype) for field in fields]
        + [pltpu.SemaphoreType.DMA((len(fields),))],
        compiler_params=limit,
        name="pack",
    )(*(pltpu.with_memory_space_constraint(field, pltpu.HBM) for field in fields))
    owners = lax.axis_size("trade")
    near_in = lax.ppermute(near, "trade", [(at, at ^ NEAR) for at in range(owners)])
    far = pl.pallas_call(
        add_shocks,
        out_shape=[message] * len(FAR),
        input_output_aliases={1 + at: at for at in range(len(FAR))},
        compiler_params=limit,
        name="add_shocks",
    )(other_shocks, *far)
    far_in = []
    for piece, pair in zip(far, FAR):
        turns = [(2 * at + core, 2 * (at ^ pair[core]) + core) for at in range(owners) for core in range(2)]
        far_in.append(lax.ppermute(piece, ("trade", "path"), turns))
    handed = [lax.ppermute(piece, "path", swap) for piece in far_in]
    netted = pl.pallas_call(
        price,
        out_shape=jax.ShapeDtypeStruct((dates_count * SLOTS_TILE, SET_DEV), jnp.float32),
        scratch_shapes=[
            pltpu.VMEM((dates_count * SLOTS_TILE, GRID), jnp.float32),
            pltpu.VMEM((dates_count * SLOTS_TILE, GRID), jnp.float32),
        ],
        compiler_params=limit,
        name="price",
    )(own, near_in, *far_in, *handed, grid)
    return netted.reshape(dates_count, SLOTS_TILE, SET_DEV).transpose(2, 0, 1)


def shards(shocks, trade_kind, *others):
    blocks, slot_count = trade_kind.shape
    by_trade = (
        lax.axis_size("trade") == SLOTS_TILE
        and lax.axis_size("path") == 2
        and shocks.shape == (2, DATES, 1, 1)
        and slot_count == 2 * SLOTS_TILE
        and blocks == SLOTS_TILE * LANES // 2
    )
    return (shards_by_trade if by_trade else shards_by_sum)(shocks, trade_kind, *others)


def solution(mesh):
    placed = (
        P("book", None, "path", "trade"),
        P(("book", "trade"), None),
        P(("book", "trade"), None),
        P(("book", "trade"), None),
        P(("book", "trade"), None),
        P(("book", "trade"), None),
        P(("book", "trade"), None),
        P(("book", "trade")),
        P(("book", "trade")),
    )
    return jax.shard_map(
        shards,
        mesh=mesh,
        in_specs=placed,
        out_specs=P(("book", "trade"), None, "path"),
        check_vma=False,
    )
```

```python
import math

import jax
import jax.numpy as jnp
from jax import lax
from jax.experimental import pallas as pl
from jax.experimental.pallas import tpu as pltpu
from jax.sharding import PartitionSpec as P

GRID = 128
SET_DEV = 32


YEAR_STEP = 0.25
FLAT_RATE = 0.03
REVERT_FAST = 0.5
REVERT_SLOW = 0.04
VOL_FAST = 0.012
VOL_SLOW = 0.009
FACTOR_CORR = -0.6
HIGHEST = lax.Precision.HIGHEST


def loading(reversion, horizon):
    return (1.0 - jnp.exp(-reversion * horizon)) / reversion


def one_variance(reversion, volatility, horizon):
    return (
        volatility**2
        / reversion**2
        * (
            horizon
            + 2.0 / reversion * jnp.exp(-reversion * horizon)
            - 0.5 / reversion * jnp.exp(-2.0 * reversion * horizon)
            - 1.5 / reversion
        )
    )


def factor_variance(horizon):
    fast_part = one_variance(REVERT_FAST, VOL_FAST, horizon)
    slow_part = one_variance(REVERT_SLOW, VOL_SLOW, horizon)
    both_rates = REVERT_FAST + REVERT_SLOW
    cross_part = (
        2.0
        * FACTOR_CORR
        * VOL_FAST
        * VOL_SLOW
        / (REVERT_FAST * REVERT_SLOW)
        * (
            horizon
            + (jnp.exp(-REVERT_FAST * horizon) - 1.0) / REVERT_FAST
            + (jnp.exp(-REVERT_SLOW * horizon) - 1.0) / REVERT_SLOW
            - (jnp.exp(-both_rates * horizon) - 1.0) / both_rates
        )
    )
    return fast_part + slow_part + cross_part


def evolve(path_shocks):
    fast_keep = math.exp(-REVERT_FAST * YEAR_STEP)
    slow_keep = math.exp(-REVERT_SLOW * YEAR_STEP)
    fast_scale = VOL_FAST * math.sqrt(
        (1.0 - math.exp(-2.0 * REVERT_FAST * YEAR_STEP)) / (2.0 * REVERT_FAST)
    )
    slow_scale = VOL_SLOW * math.sqrt(
        (1.0 - math.exp(-2.0 * REVERT_SLOW * YEAR_STEP)) / (2.0 * REVERT_SLOW)
    )
    mixing = math.sqrt(1.0 - FACTOR_CORR**2)
    fast_state = jnp.zeros(path_shocks.shape[2:], jnp.float32)
    slow_state = jnp.zeros(path_shocks.shape[2:], jnp.float32)
    fast_path = []
    slow_path = []
    for period in range(path_shocks.shape[1]):
        fast_state = fast_state * fast_keep + fast_scale * path_shocks[0, period]
        slow_state = slow_state * slow_keep + slow_scale * (
            FACTOR_CORR * path_shocks[0, period] + mixing * path_shocks[1, period]
        )
        fast_path.append(fast_state)
        slow_path.append(slow_state)
    return jnp.stack([jnp.stack(fast_path), jnp.stack(slow_path)])


def discount_table(states):
    dates_count = states.shape[1]
    maturity = lax.broadcasted_iota(jnp.int32, (GRID, 1, 1), 0).astype(jnp.float32) * YEAR_STEP
    valued = (lax.broadcasted_iota(jnp.int32, (1, dates_count, 1), 1) + 1).astype(
        jnp.float32
    ) * YEAR_STEP
    horizon = maturity - valued
    log_front = -FLAT_RATE * horizon + 0.5 * (
        factor_variance(horizon) - factor_variance(maturity) + factor_variance(valued)
    )
    return jnp.exp(
        log_front
        - loading(REVERT_FAST, horizon) * states[0][None]
        - loading(REVERT_SLOW, horizon) * states[1][None]
    )


def price_blocks(
    trade_kind,
    cash_start,
    cash_count,
    strike,
    normal_vol,
    notional,
    block_count,
    discounts,
    dates_count,
):
    groups, slot_count = cash_start.shape
    cash_nodes = lax.broadcasted_iota(jnp.int32, (1, 1, GRID), 2)
    first_node = cash_start[:, :, None]
    last_node = (cash_start + cash_count)[:, :, None]
    accrual = jnp.where(
        (cash_nodes > first_node) & (cash_nodes <= last_node), YEAR_STEP, 0.0
    ).astype(jnp.float32)
    endpoints = (
        jnp.where(cash_nodes == first_node, 1.0, 0.0) - jnp.where(cash_nodes == last_node, 1.0, 0.0)
    ).astype(jnp.float32)
    weights = jnp.concatenate([accrual, endpoints], axis=0).reshape(2 * groups * slot_count, GRID)
    products = jnp.dot(weights, discounts, precision=HIGHEST, preferred_element_type=jnp.float32)
    products = products.reshape(2, groups, slot_count, dates_count, -1)
    annuity = products[0]
    float_leg = products[1]
    swap_rate = float_leg / annuity
    valued = (lax.broadcasted_iota(jnp.int32, (1, 1, dates_count, 1), 2) + 1).astype(
        jnp.float32
    ) * YEAR_STEP
    expiry = cash_start.astype(jnp.float32)[:, :, None, None] * YEAR_STEP
    spread = normal_vol[:, :, None, None] * jnp.sqrt(expiry - valued)
    moneyness = swap_rate - strike[:, :, None, None]
    standard = moneyness / spread
    normal_cdf = 0.5 * (1.0 + jax.scipy.special.erf(standard * (1.0 / math.sqrt(2.0))))
    normal_pdf = jnp.exp(-0.5 * standard * standard) * (1.0 / math.sqrt(2.0 * math.pi))
    offset = jnp.where(trade_kind == 1, 1.0, jnp.where(trade_kind == 2, 0.5, 0.0))[:, :, None, None]
    factor = (jnp.where(trade_kind == 2, 2.0, 1.0) * notional)[:, :, None, None]
    trade_value = factor * annuity * (moneyness * (normal_cdf - offset) + spread * normal_pdf)
    occupied = lax.broadcasted_iota(jnp.int32, (groups, slot_count), 1) < block_count[:, None]
    trade_value = jnp.where(occupied[:, :, None, None], trade_value, 0.0)
    return jnp.sum(trade_value, axis=1).reshape(groups, -1)


def price_all(fields, discounts, dates_count):
    block_rows = fields[0].shape[0]
    group_size = max(32, block_rows // 16)
    turns = block_rows // group_size

    def regroup(array):
        return array.reshape((turns, group_size) + array.shape[1:])

    def one_group(pieces):
        return price_blocks(
            pieces[0],
            pieces[1],
            pieces[2],
            pieces[3],
            pieces[4],
            pieces[5],
            pieces[6],
            discounts,
            dates_count,
        )

    totals = lax.map(one_group, tuple((regroup(field) for field in fields)))
    return totals.reshape(block_rows, -1)


def shards_by_sum(
    shocks, trade_kind, cash_start, cash_count, strike, normal_vol, notional, block_count, block_set
):
    dates_count = shocks.shape[1]
    own_states = evolve(shocks.reshape(2, dates_count, -1))
    gathered = lax.all_gather(own_states, "trade", axis=2, tiled=True)
    discounts = discount_table(gathered)
    discounts = discounts.reshape(GRID, -1)
    block_total = price_all(
        (trade_kind, cash_start, cash_count, strike, normal_vol, notional, block_count),
        discounts,
        dates_count,
    )
    set_index = lax.broadcasted_iota(jnp.int32, (SET_DEV * lax.axis_size("trade"), 1), 0)
    one_hot = (set_index == block_set[None, :]).astype(jnp.float32)
    netted = lax.psum_scatter(
        jnp.dot(one_hot, block_total, precision=HIGHEST, preferred_element_type=jnp.float32),
        "trade",
        scatter_dimension=0,
        tiled=True,
    )
    return jnp.maximum(netted, 0.0).reshape(SET_DEV, dates_count, -1)


SLOTS_TILE = 8
LANES = 128
FIELDS = 6
ROWS = (FIELDS + 1) * SLOTS_TILE
INPUTS = range(9)
NEAR = 1
FAR = ((2, 4), (3, 6), (5, 7))
DATES = 2
VMEM_BYTES = 8 * 2**20

TAIL = (
    -1.325748085975647,
    -1.8081518411636353,
    -0.41172587871551514,
    -0.042724475264549255,
    0.0027914412785321474,
    0.00040712140616960824,
    -0.00013435240543913096,
    1.5000393432273995e-05,
    -6.33199476851587e-07,
)


def iota(shape, dimension):
    return lax.broadcasted_iota(jnp.int32, shape, dimension)


def offsets(core):
    return [NEAR] + [jnp.where(core == 0, first, second) for first, second in FAR]


def pack(*refs):
    count_of = len(INPUTS)
    sources, outs = refs[:count_of], refs[count_of : count_of + 2 + len(FAR)]
    grid = refs[count_of + 2 + len(FAR)]
    held, arrived = refs[count_of + 3 + len(FAR) : -1], refs[-1]
    copies = [
        pltpu.make_async_copy(source, target, arrived.at[at])
        for at, (source, target) in enumerate(zip(sources, held))
    ]
    for copy in copies:
        copy.start()
    for at, rows in enumerate(curve_rows()):
        grid[at] = rows
    me, core = lax.axis_index("trade"), lax.axis_index("path")
    half = LANES // 2
    low = iota((SLOTS_TILE, LANES), 1) < half
    row, lane = iota((SLOTS_TILE, LANES), 0), iota((SLOTS_TILE, LANES), 1)
    for copy in copies:
        copy.wait()
    kind, start, count, strike, vol, notional, live, group, shocks = held
    own_shocks = jnp.zeros((SLOTS_TILE, LANES), jnp.float32)
    for factor in range(2):
        for date in range(DATES):
            value = jnp.broadcast_to(shocks[factor : factor + 1, date : date + 1], (SLOTS_TILE, LANES))
            own_shocks = jnp.where(lane == factor * DATES + date, value, own_shocks)
    for out, offset in zip(outs, [0] + offsets(core)):
        owner = me ^ offset
        cut = pl.ds(pl.multiple_of(owner // 2 * LANES, LANES), LANES)
        odd = owner % 2

        def both(low_half, high_half):
            return jnp.where(
                low, pltpu.roll(low_half, half * odd, 1), pltpu.roll(high_half, half * (1 - odd), 1)
            )

        def field(ref):
            return both(ref[:SLOTS_TILE, cut], ref[SLOTS_TILE:, cut])

        lives = jnp.broadcast_to(live[:, cut], (SLOTS_TILE, LANES))
        sets = jnp.broadcast_to(group[:, cut], (SLOTS_TILE, LANES))
        slot = row + jnp.where(low, 0, SLOTS_TILE)
        first, kinds = field(start), field(kind)
        size = jnp.where(kinds == 2, 2.0, 1.0) * field(notional)
        tiles = (
            first.astype(jnp.float32),
            (first + field(count)).astype(jnp.float32),
            field(strike),
            field(vol),
            jnp.where(slot < both(lives, lives), size, 0.0),
            jnp.where(kinds == 1, 1.0, jnp.where(kinds == 2, 0.5, 0.0)),
            jnp.where(row == 0, (both(sets, sets) - owner * SET_DEV).astype(jnp.float32), own_shocks),
        )
        for at, tile in enumerate(tiles):
            out[at * SLOTS_TILE : (at + 1) * SLOTS_TILE, :] = tile


def add_shocks(shocks, *refs):
    core = lax.axis_index("path")
    lane = iota((1, LANES), 1)
    line = jnp.zeros((1, LANES), jnp.float32)
    for factor in range(2):
        for date in range(DATES):
            value = jnp.broadcast_to(shocks[factor : factor + 1, date : date + 1], (1, LANES))
            line = jnp.where(lane == factor * DATES + date, value, line)
    for ref in refs[len(FAR) :]:
        ref[pl.ds(FIELDS * SLOTS_TILE + 2 - core, 1), :] = line


def split(values, count):
    parts = []
    for _ in range(count):
        part = values.astype(jnp.bfloat16)
        parts.append(part)
        values = values - part.astype(jnp.float32)
    return jnp.concatenate(parts, axis=0)


def add_parts(product, count):
    rows = product.shape[0] // count
    total = product[(count - 1) * rows :]
    for part in range(count - 2, -1, -1):
        total = total + product[part * rows : (part + 1) * rows]
    return total


def curve_rows():
    node = iota((SLOTS_TILE, GRID), 1).astype(jnp.float32) * YEAR_STEP
    row = iota((SLOTS_TILE, GRID), 0)
    valued = jnp.where(row < DATES + 1, row, 1).astype(jnp.float32) * YEAR_STEP
    horizon = node - valued
    front = -FLAT_RATE * horizon + 0.5 * (
        factor_variance(horizon) - factor_variance(node) + factor_variance(valued)
    )
    return front, loading(REVERT_FAST, horizon), loading(REVERT_SLOW, horizon)


def tables(shocks, grid):
    states = evolve(shocks)
    discounts = []
    for date in range(DATES):
        front, fast, slow = (grid[at, date + 1 : date + 2, :] for at in range(3))
        discounts.append(jnp.exp(front - fast * states[0, date] - slow * states[1, date]))
    both = jnp.concatenate(discounts, axis=0)
    mid = GRID // 4
    source, target = iota((GRID, GRID), 0), iota((GRID, GRID), 1)
    weights = jnp.where((source > mid) & (source <= target), YEAR_STEP, 0.0) - jnp.where(
        (source <= mid) & (source > target), YEAR_STEP, 0.0
    )
    sums = jnp.dot(split(both, 3), weights.astype(jnp.bfloat16), preferred_element_type=jnp.float32)
    return both, add_parts(sums, 3)


def price_source(ref, discount, running, masks):
    def field(at):
        return ref[at * SLOTS_TILE : (at + 1) * SLOTS_TILE, :]

    def look_up(table, at, index):
        row = jnp.broadcast_to(table[at : at + 1, :], (SLOTS_TILE, LANES))
        return jnp.take_along_axis(row, index, axis=1, mode="promise_in_bounds")

    first, last = field(0), field(1)
    first_node, last_node = first.astype(jnp.int32), last.astype(jnp.int32)
    strike, vol, size, offset = field(2), field(3), field(4), field(5)
    tilt = 0.5 - offset
    totals = []
    for date in range(DATES):
        spread = vol * jnp.sqrt(first * YEAR_STEP - (date + 1) * YEAR_STEP)
        inverse = 1.0 / spread
        scale = size * spread
        hurdle = strike * inverse
        rows = range(date * SLOTS_TILE, (date + 1) * SLOTS_TILE)
        starts = [(look_up(discount, at, first_node), look_up(running, at, first_node)) for at in rows]
        ends = [(look_up(discount, at, last_node), look_up(running, at, last_node)) for at in rows]
        values = []
        for (curve_start, sum_start), (curve_end, sum_end) in zip(starts, ends):
            float_leg, annuity = curve_start - curve_end, sum_end - sum_start
            standard = float_leg * pl.reciprocal(annuity) * inverse - hurdle
            size_of = jnp.abs(standard)
            power = jnp.full_like(size_of, TAIL[-1])
            for term in TAIL[-2::-1]:
                power = power * size_of + term
            values.append(scale * annuity * (0.5 * size_of + tilt * standard + jnp.exp2(power)))
        for bit, mask in zip((1, 2, 4), masks):
            values = [
                jnp.where(mask, a, b) + pltpu.roll(jnp.where(mask, b, a), bit, 0)
                for a, b in zip(values[::2], values[1::2])
            ]
        totals.append(values[0])
    return jnp.concatenate(totals, axis=0)


def price(*refs):
    refs, (grid, out, discount, running) = refs[:-4], refs[-4:]
    extra = FIELDS * SLOTS_TILE
    me, core = lax.axis_index("trade"), lax.axis_index("path")
    row = iota((SLOTS_TILE, LANES), 0)
    lines = jnp.zeros((SLOTS_TILE, LANES), jnp.float32)
    for ref, offset in zip(refs, [0] + offsets(core) + offsets(1 - core)[1:]):
        line = jnp.broadcast_to(ref[pl.ds(extra + 1 + core, 1), :], (SLOTS_TILE, LANES))
        lines = jnp.where(row == (me ^ offset), line, lines)
    shocks = jnp.stack(
        [
            jnp.stack(
                [
                    jnp.broadcast_to(lines[:, at : at + 1], (SLOTS_TILE, LANES))
                    for at in range(factor * DATES, (factor + 1) * DATES)
                ]
            )
            for factor in range(2)
        ]
    )
    discount[...], running[...] = tables(shocks, grid)
    masks = [(row & bit) == 0 for bit in (1, 2, 4)]
    set_index = iota((SET_DEV, LANES), 0).astype(jnp.float32)
    one_hot = jnp.concatenate(
        [(set_index == ref[extra : extra + 1, :]).astype(jnp.bfloat16) for ref in refs], axis=1
    )
    totals = jnp.concatenate([price_source(ref, discount, running, masks) for ref in refs], axis=1)
    netted = lax.dot_general(
        split(totals, 3), one_hot, (((1,), (1,)), ((), ())), preferred_element_type=jnp.float32
    )
    out[...] = jnp.maximum(add_parts(netted, 3), 0.0)


def shards_by_trade(
    shocks, trade_kind, cash_start, cash_count, strike, normal_vol, notional, block_count, block_set
):
    dates_count = shocks.shape[1]
    own_shocks = shocks.reshape(2, dates_count)
    swap = [(0, 1), (1, 0)]
    other_shocks = lax.ppermute(shocks, "path", swap).reshape(2, dates_count)
    fields = (
        trade_kind.T,
        cash_start.T,
        cash_count.T,
        strike.T,
        normal_vol.T,
        notional.T,
        block_count.reshape(1, -1),
        block_set.reshape(1, -1),
        own_shocks,
    )
    message = jax.ShapeDtypeStruct((ROWS, LANES), jnp.float32)
    limit = pltpu.CompilerParams(vmem_limit_bytes=VMEM_BYTES)
    own, near, *far, grid = pl.pallas_call(
        pack,
        out_shape=[message] * (2 + len(FAR)) + [jax.ShapeDtypeStruct((3, SLOTS_TILE, GRID), jnp.float32)],
        in_specs=[pl.BlockSpec(memory_space=pltpu.HBM)] * len(fields),
        scratch_shapes=[pltpu.VMEM(field.shape, field.dtype) for field in fields]
        + [pltpu.SemaphoreType.DMA((len(fields),))],
        compiler_params=limit,
        name="pack",
    )(*(pltpu.with_memory_space_constraint(field, pltpu.HBM) for field in fields))
    owners = lax.axis_size("trade")
    near_in = lax.ppermute(near, "trade", [(at, at ^ NEAR) for at in range(owners)])
    far = pl.pallas_call(
        add_shocks,
        out_shape=[message] * len(FAR),
        input_output_aliases={1 + at: at for at in range(len(FAR))},
        compiler_params=limit,
        name="add_shocks",
    )(other_shocks, *far)
    far_in = []
    for piece, pair in zip(far, FAR):
        turns = [(2 * at + core, 2 * (at ^ pair[core]) + core) for at in range(owners) for core in range(2)]
        far_in.append(lax.ppermute(piece, ("trade", "path"), turns))
    handed = [lax.ppermute(piece, "path", swap) for piece in far_in]
    netted = pl.pallas_call(
        price,
        out_shape=jax.ShapeDtypeStruct((dates_count * SLOTS_TILE, SET_DEV), jnp.float32),
        scratch_shapes=[
            pltpu.VMEM((dates_count * SLOTS_TILE, GRID), jnp.float32),
            pltpu.VMEM((dates_count * SLOTS_TILE, GRID), jnp.float32),
        ],
        compiler_params=limit,
        name="price",
    )(own, near_in, *far_in, *handed, grid)
    return netted.reshape(dates_count, SLOTS_TILE, SET_DEV).transpose(2, 0, 1)


def shards(shocks, trade_kind, *others):
    blocks, slot_count = trade_kind.shape
    by_trade = (
        lax.axis_size("trade") == SLOTS_TILE
        and lax.axis_size("path") == 2
        and shocks.shape == (2, DATES, 1, 1)
        and slot_count == 2 * SLOTS_TILE
        and blocks == SLOTS_TILE * LANES // 2
    )
    return (shards_by_trade if by_trade else shards_by_sum)(shocks, trade_kind, *others)


def solution(mesh):
    placed = (
        P("book", None, "path", "trade"),
        P(("book", "trade"), None),
        P(("book", "trade"), None),
        P(("book", "trade"), None),
        P(("book", "trade"), None),
        P(("book", "trade"), None),
        P(("book", "trade"), None),
        P(("book", "trade")),
        P(("book", "trade")),
    )
    return jax.shard_map(
        shards,
        mesh=mesh,
        in_specs=placed,
        out_specs=P(("book", "trade"), None, "path"),
        check_vma=False,
    )
```

```python
import math

import jax
import jax.numpy as jnp
from jax import lax
from jax.experimental import pallas as pl
from jax.experimental.pallas import tpu as pltpu
from jax.sharding import PartitionSpec as P

GRID = 128
SET_DEV = 32


YEAR_STEP = 0.25
FLAT_RATE = 0.03
REVERT_FAST = 0.5
REVERT_SLOW = 0.04
VOL_FAST = 0.012
VOL_SLOW = 0.009
FACTOR_CORR = -0.6
HIGHEST = lax.Precision.HIGHEST


def loading(reversion, horizon):
    return (1.0 - jnp.exp(-reversion * horizon)) / reversion


def one_variance(reversion, volatility, horizon):
    return (
        volatility**2
        / reversion**2
        * (
            horizon
            + 2.0 / reversion * jnp.exp(-reversion * horizon)
            - 0.5 / reversion * jnp.exp(-2.0 * reversion * horizon)
            - 1.5 / reversion
        )
    )


def factor_variance(horizon):
    fast_part = one_variance(REVERT_FAST, VOL_FAST, horizon)
    slow_part = one_variance(REVERT_SLOW, VOL_SLOW, horizon)
    both_rates = REVERT_FAST + REVERT_SLOW
    cross_part = (
        2.0
        * FACTOR_CORR
        * VOL_FAST
        * VOL_SLOW
        / (REVERT_FAST * REVERT_SLOW)
        * (
            horizon
            + (jnp.exp(-REVERT_FAST * horizon) - 1.0) / REVERT_FAST
            + (jnp.exp(-REVERT_SLOW * horizon) - 1.0) / REVERT_SLOW
            - (jnp.exp(-both_rates * horizon) - 1.0) / both_rates
        )
    )
    return fast_part + slow_part + cross_part


def evolve(path_shocks):
    fast_keep = math.exp(-REVERT_FAST * YEAR_STEP)
    slow_keep = math.exp(-REVERT_SLOW * YEAR_STEP)
    fast_scale = VOL_FAST * math.sqrt(
        (1.0 - math.exp(-2.0 * REVERT_FAST * YEAR_STEP)) / (2.0 * REVERT_FAST)
    )
    slow_scale = VOL_SLOW * math.sqrt(
        (1.0 - math.exp(-2.0 * REVERT_SLOW * YEAR_STEP)) / (2.0 * REVERT_SLOW)
    )
    mixing = math.sqrt(1.0 - FACTOR_CORR**2)
    fast_state = jnp.zeros(path_shocks.shape[2:], jnp.float32)
    slow_state = jnp.zeros(path_shocks.shape[2:], jnp.float32)
    fast_path = []
    slow_path = []
    for period in range(path_shocks.shape[1]):
        fast_state = fast_state * fast_keep + fast_scale * path_shocks[0, period]
        slow_state = slow_state * slow_keep + slow_scale * (
            FACTOR_CORR * path_shocks[0, period] + mixing * path_shocks[1, period]
        )
        fast_path.append(fast_state)
        slow_path.append(slow_state)
    return jnp.stack([jnp.stack(fast_path), jnp.stack(slow_path)])


def discount_table(states):
    dates_count = states.shape[1]
    maturity = lax.broadcasted_iota(jnp.int32, (GRID, 1, 1), 0).astype(jnp.float32) * YEAR_STEP
    valued = (lax.broadcasted_iota(jnp.int32, (1, dates_count, 1), 1) + 1).astype(
        jnp.float32
    ) * YEAR_STEP
    horizon = maturity - valued
    log_front = -FLAT_RATE * horizon + 0.5 * (
        factor_variance(horizon) - factor_variance(maturity) + factor_variance(valued)
    )
    return jnp.exp(
        log_front
        - loading(REVERT_FAST, horizon) * states[0][None]
        - loading(REVERT_SLOW, horizon) * states[1][None]
    )


def price_blocks(
    trade_kind,
    cash_start,
    cash_count,
    strike,
    normal_vol,
    notional,
    block_count,
    discounts,
    dates_count,
):
    groups, slot_count = cash_start.shape
    cash_nodes = lax.broadcasted_iota(jnp.int32, (1, 1, GRID), 2)
    first_node = cash_start[:, :, None]
    last_node = (cash_start + cash_count)[:, :, None]
    accrual = jnp.where(
        (cash_nodes > first_node) & (cash_nodes <= last_node), YEAR_STEP, 0.0
    ).astype(jnp.float32)
    endpoints = (
        jnp.where(cash_nodes == first_node, 1.0, 0.0) - jnp.where(cash_nodes == last_node, 1.0, 0.0)
    ).astype(jnp.float32)
    weights = jnp.concatenate([accrual, endpoints], axis=0).reshape(2 * groups * slot_count, GRID)
    products = jnp.dot(weights, discounts, precision=HIGHEST, preferred_element_type=jnp.float32)
    products = products.reshape(2, groups, slot_count, dates_count, -1)
    annuity = products[0]
    float_leg = products[1]
    swap_rate = float_leg / annuity
    valued = (lax.broadcasted_iota(jnp.int32, (1, 1, dates_count, 1), 2) + 1).astype(
        jnp.float32
    ) * YEAR_STEP
    expiry = cash_start.astype(jnp.float32)[:, :, None, None] * YEAR_STEP
    spread = normal_vol[:, :, None, None] * jnp.sqrt(expiry - valued)
    moneyness = swap_rate - strike[:, :, None, None]
    standard = moneyness / spread
    normal_cdf = 0.5 * (1.0 + jax.scipy.special.erf(standard * (1.0 / math.sqrt(2.0))))
    normal_pdf = jnp.exp(-0.5 * standard * standard) * (1.0 / math.sqrt(2.0 * math.pi))
    offset = jnp.where(trade_kind == 1, 1.0, jnp.where(trade_kind == 2, 0.5, 0.0))[:, :, None, None]
    factor = (jnp.where(trade_kind == 2, 2.0, 1.0) * notional)[:, :, None, None]
    trade_value = factor * annuity * (moneyness * (normal_cdf - offset) + spread * normal_pdf)
    occupied = lax.broadcasted_iota(jnp.int32, (groups, slot_count), 1) < block_count[:, None]
    trade_value = jnp.where(occupied[:, :, None, None], trade_value, 0.0)
    return jnp.sum(trade_value, axis=1).reshape(groups, -1)


def price_all(fields, discounts, dates_count):
    block_rows = fields[0].shape[0]
    group_size = max(32, block_rows // 16)
    turns = block_rows // group_size

    def regroup(array):
        return array.reshape((turns, group_size) + array.shape[1:])

    def one_group(pieces):
        return price_blocks(
            pieces[0],
            pieces[1],
            pieces[2],
            pieces[3],
            pieces[4],
            pieces[5],
            pieces[6],
            discounts,
            dates_count,
        )

    totals = lax.map(one_group, tuple((regroup(field) for field in fields)))
    return totals.reshape(block_rows, -1)


def shards_by_sum(
    shocks, trade_kind, cash_start, cash_count, strike, normal_vol, notional, block_count, block_set
):
    dates_count = shocks.shape[1]
    own_states = evolve(shocks.reshape(2, dates_count, -1))
    gathered = lax.all_gather(own_states, "trade", axis=2, tiled=True)
    discounts = discount_table(gathered)
    discounts = discounts.reshape(GRID, -1)
    block_total = price_all(
        (trade_kind, cash_start, cash_count, strike, normal_vol, notional, block_count),
        discounts,
        dates_count,
    )
    set_index = lax.broadcasted_iota(jnp.int32, (SET_DEV * lax.axis_size("trade"), 1), 0)
    one_hot = (set_index == block_set[None, :]).astype(jnp.float32)
    netted = lax.psum_scatter(
        jnp.dot(one_hot, block_total, precision=HIGHEST, preferred_element_type=jnp.float32),
        "trade",
        scatter_dimension=0,
        tiled=True,
    )
    return jnp.maximum(netted, 0.0).reshape(SET_DEV, dates_count, -1)


SLOTS_TILE = 8
LANES = 128
FIELDS = 6
ROWS = (FIELDS + 1) * SLOTS_TILE
INPUTS = range(9)
NEAR = 1
FAR = ((2, 4), (3, 6), (5, 7))
SLOTS = 8
EARLY = 6
DATES = 2
VMEM_BYTES = 8 * 2**20

TAIL = (
    -1.325748085975647,
    -1.8081518411636353,
    -0.41172587871551514,
    -0.042724475264549255,
    0.0027914412785321474,
    0.00040712140616960824,
    -0.00013435240543913096,
    1.5000393432273995e-05,
    -6.33199476851587e-07,
)


def iota(shape, dimension):
    return lax.broadcasted_iota(jnp.int32, shape, dimension)


def offsets(core):
    return [NEAR] + [jnp.where(core == 0, first, second) for first, second in FAR]


def slot_offsets(core):
    near, *far = offsets(core)
    *handed, last = offsets(1 - core)[1:]
    return [0, *far, *handed, near, last]


def pack(*refs):
    count_of = len(INPUTS)
    sources, outs = refs[:count_of], refs[count_of : count_of + 2 + len(FAR)]
    grid = refs[count_of + 2 + len(FAR)]
    held, arrived = refs[count_of + 3 + len(FAR) : -1], refs[-1]
    copies = [
        pltpu.make_async_copy(source, target, arrived.at[at])
        for at, (source, target) in enumerate(zip(sources, held))
    ]
    for copy in copies:
        copy.start()
    for at, rows in enumerate(curve_rows()):
        grid[at] = rows
    me, core = lax.axis_index("trade"), lax.axis_index("path")
    half = LANES // 2
    low = iota((SLOTS_TILE, LANES), 1) < half
    row, lane = iota((SLOTS_TILE, LANES), 0), iota((SLOTS_TILE, LANES), 1)
    for copy in copies:
        copy.wait()
    kind, start, count, strike, vol, notional, live, group, shocks = held
    own_shocks = jnp.zeros((SLOTS_TILE, LANES), jnp.float32)
    for factor in range(2):
        for date in range(DATES):
            value = jnp.broadcast_to(shocks[factor : factor + 1, date : date + 1], (SLOTS_TILE, LANES))
            own_shocks = jnp.where(lane == factor * DATES + date, value, own_shocks)
    for out, offset in zip(outs, [0] + offsets(core)):
        owner = me ^ offset
        cut = pl.ds(pl.multiple_of(owner // 2 * LANES, LANES), LANES)
        odd = owner % 2

        def both(low_half, high_half):
            return jnp.where(
                low, pltpu.roll(low_half, half * odd, 1), pltpu.roll(high_half, half * (1 - odd), 1)
            )

        def field(ref):
            return both(ref[:SLOTS_TILE, cut], ref[SLOTS_TILE:, cut])

        lives = jnp.broadcast_to(live[:, cut], (SLOTS_TILE, LANES))
        sets = jnp.broadcast_to(group[:, cut], (SLOTS_TILE, LANES))
        slot = row + jnp.where(low, 0, SLOTS_TILE)
        first, kinds = field(start), field(kind)
        size = jnp.where(kinds == 2, 2.0, 1.0) * field(notional)
        tiles = (
            first.astype(jnp.float32),
            (first + field(count)).astype(jnp.float32),
            field(strike),
            field(vol),
            jnp.where(slot < both(lives, lives), size, 0.0),
            jnp.where(kinds == 1, 1.0, jnp.where(kinds == 2, 0.5, 0.0)),
            jnp.where(row == 0, (both(sets, sets) - owner * SET_DEV).astype(jnp.float32), own_shocks),
        )
        for at, tile in enumerate(tiles):
            out[at * SLOTS_TILE : (at + 1) * SLOTS_TILE, :] = tile
    outs[1][ROWS:, :] = jnp.zeros((SLOTS_TILE, LANES), jnp.float32)


def add_shocks(shocks, *refs):
    core = lax.axis_index("path")
    lane = iota((1, LANES), 1)
    line = jnp.zeros((1, LANES), jnp.float32)
    for factor in range(2):
        for date in range(DATES):
            value = jnp.broadcast_to(shocks[factor : factor + 1, date : date + 1], (1, LANES))
            line = jnp.where(lane == factor * DATES + date, value, line)
    for ref in refs[len(FAR) :]:
        ref[pl.ds(FIELDS * SLOTS_TILE + 2 - core, 1), :] = line


def split(values, count):
    parts = []
    for _ in range(count):
        part = values.astype(jnp.bfloat16)
        parts.append(part)
        values = values - part.astype(jnp.float32)
    return jnp.concatenate(parts, axis=0)


def add_parts(product, count):
    rows = product.shape[0] // count
    total = product[(count - 1) * rows :]
    for part in range(count - 2, -1, -1):
        total = total + product[part * rows : (part + 1) * rows]
    return total


def curve_rows():
    node = iota((SLOTS_TILE, GRID), 1).astype(jnp.float32) * YEAR_STEP
    row = iota((SLOTS_TILE, GRID), 0)
    valued = jnp.where(row < DATES + 1, row, 1).astype(jnp.float32) * YEAR_STEP
    horizon = node - valued
    front = -FLAT_RATE * horizon + 0.5 * (
        factor_variance(horizon) - factor_variance(node) + factor_variance(valued)
    )
    return front, loading(REVERT_FAST, horizon), loading(REVERT_SLOW, horizon)


def tables(shocks, grid):
    states = evolve(shocks)
    discounts = []
    for date in range(DATES):
        front, fast, slow = (grid[at, date + 1 : date + 2, :] for at in range(3))
        discounts.append(jnp.exp(front - fast * states[0, date] - slow * states[1, date]))
    both = jnp.concatenate(discounts, axis=0)
    mid = GRID // 4
    source, target = iota((GRID, GRID), 0), iota((GRID, GRID), 1)
    weights = jnp.where((source > mid) & (source <= target), YEAR_STEP, 0.0) - jnp.where(
        (source <= mid) & (source > target), YEAR_STEP, 0.0
    )
    sums = jnp.dot(split(both, 3), weights.astype(jnp.bfloat16), preferred_element_type=jnp.float32)
    return both, add_parts(sums, 3)


def price_source(ref, discount, running, slots):
    def field(at):
        return ref[at * SLOTS_TILE : (at + 1) * SLOTS_TILE, :]

    def look_up(table, at, index):
        row = jnp.broadcast_to(table[at : at + 1, :], (SLOTS_TILE, LANES))
        return jnp.take_along_axis(row, index, axis=1, mode="promise_in_bounds")

    def merge(first, second, bit):
        if first is None and second is None:
            return None
        zero = jnp.zeros((SLOTS_TILE, LANES), jnp.float32)
        first = zero if first is None else first
        second = zero if second is None else second
        mask = (iota((SLOTS_TILE, LANES), 0) & bit) == 0
        return jnp.where(mask, first, second) + pltpu.roll(jnp.where(mask, second, first), bit, 0)

    first, last = field(0), field(1)
    first_node, last_node = first.astype(jnp.int32), last.astype(jnp.int32)
    strike, vol, size, offset = field(2), field(3), field(4), field(5)
    tilt = 0.5 - offset
    totals = []
    for date in range(DATES):
        spread = vol * jnp.sqrt(first * YEAR_STEP - (date + 1) * YEAR_STEP)
        inverse = 1.0 / spread
        scale = size * spread
        hurdle = strike * inverse
        rows = [date * SLOTS + slot for slot in slots]
        starts = [(look_up(discount, at, first_node), look_up(running, at, first_node)) for at in rows]
        ends = [(look_up(discount, at, last_node), look_up(running, at, last_node)) for at in rows]
        values = [None] * SLOTS
        for slot, (curve_start, sum_start), (curve_end, sum_end) in zip(slots, starts, ends):
            float_leg, annuity = curve_start - curve_end, sum_end - sum_start
            standard = float_leg * pl.reciprocal(annuity) * inverse - hurdle
            size_of = jnp.abs(standard)
            power = jnp.full_like(size_of, TAIL[-1])
            for term in TAIL[-2::-1]:
                power = power * size_of + term
            values[slot] = scale * annuity * (0.5 * size_of + tilt * standard + jnp.exp2(power))
        for bit in (1, 2, 4):
            values = [merge(a, b, bit) for a, b in zip(values[::2], values[1::2])]
        totals.append(values[0])
    return jnp.concatenate(totals, axis=0)


def set_tables(refs, grid, discount, running):
    line = FIELDS * SLOTS_TILE + 1 + lax.axis_index("path")
    lines = jnp.concatenate(
        [ref[pl.ds(line, 1), :] for ref in refs] + [jnp.zeros((1, LANES), jnp.float32)] * (SLOTS - len(refs)), axis=0
    )
    shocks = [jnp.broadcast_to(lines[:, at : at + 1], (SLOTS, LANES)) for at in range(2 * DATES)]
    shocks = jnp.stack([jnp.stack(shocks[:DATES]), jnp.stack(shocks[DATES:])])
    discount[...], running[...] = tables(shocks, grid)


def net(refs, totals):
    extra = FIELDS * SLOTS_TILE
    set_index = iota((SET_DEV, LANES), 0).astype(jnp.float32)
    one_hot = jnp.concatenate(
        [(set_index == ref[extra : extra + 1, :]).astype(jnp.bfloat16) for ref in refs], axis=1
    )
    netted = lax.dot_general(
        split(jnp.concatenate(totals, axis=1), 3),
        one_hot,
        (((1,), (1,)), ((), ())),
        preferred_element_type=jnp.float32,
    )
    return add_parts(netted, 3)


def price_early(*refs):
    refs, (grid, out, discount, running) = refs[:-4], refs[-4:]
    set_tables(refs, grid, discount, running)
    out[...] = net(refs, [price_source(ref, discount, running, range(EARLY)) for ref in refs])


def price_late(*refs):
    refs, (grid, early, out, discount, running) = refs[:-5], refs[-5:]
    set_tables(refs, grid, discount, running)
    totals = [
        price_source(ref, discount, running, range(EARLY if at < EARLY else 0, SLOTS)) for at, ref in enumerate(refs)
    ]
    netted = jnp.maximum(net(refs, totals) + early[...], 0.0)
    me = lax.axis_index("trade")
    for slot, offset in enumerate(slot_offsets(lax.axis_index("path"))):
        for date in range(DATES):
            at = date * SLOTS + slot
            out[pl.ds(date * SLOTS + (me ^ offset), 1), :] = netted[at : at + 1, :]


def shards_by_trade(
    shocks, trade_kind, cash_start, cash_count, strike, normal_vol, notional, block_count, block_set
):
    dates_count = shocks.shape[1]
    own_shocks = shocks.reshape(2, dates_count)
    swap = [(0, 1), (1, 0)]
    other_shocks = lax.ppermute(shocks, "path", swap).reshape(2, dates_count)
    fields = (
        trade_kind.T,
        cash_start.T,
        cash_count.T,
        strike.T,
        normal_vol.T,
        notional.T,
        block_count.reshape(1, -1),
        block_set.reshape(1, -1),
        own_shocks,
    )
    message = jax.ShapeDtypeStruct((ROWS, LANES), jnp.float32)
    near_message = jax.ShapeDtypeStruct((ROWS + SLOTS_TILE, LANES), jnp.float32)
    limit = pltpu.CompilerParams(vmem_limit_bytes=VMEM_BYTES)
    own, near, *far, grid = pl.pallas_call(
        pack,
        out_shape=[message, near_message] + [message] * len(FAR) + [jax.ShapeDtypeStruct((3, SLOTS_TILE, GRID), jnp.float32)],
        in_specs=[pl.BlockSpec(memory_space=pltpu.HBM)] * len(fields),
        scratch_shapes=[pltpu.VMEM(field.shape, field.dtype) for field in fields]
        + [pltpu.SemaphoreType.DMA((len(fields),))],
        compiler_params=limit,
        name="pack",
    )(*(pltpu.with_memory_space_constraint(field, pltpu.HBM) for field in fields))
    owners = lax.axis_size("trade")
    near_in = lax.ppermute(near, "trade", [(at, at ^ NEAR) for at in range(owners)])
    far = pl.pallas_call(
        add_shocks,
        out_shape=[message] * len(FAR),
        input_output_aliases={1 + at: at for at in range(len(FAR))},
        compiler_params=limit,
        name="add_shocks",
    )(other_shocks, *far)
    far_in = []
    for piece, pair in zip(far, FAR):
        turns = [(2 * at + core, 2 * (at ^ pair[core]) + core) for at in range(owners) for core in range(2)]
        far_in.append(lax.ppermute(piece, ("trade", "path"), turns))
    handed = [lax.ppermute(piece, "path", swap) for piece in far_in]
    result = jax.ShapeDtypeStruct((dates_count * SLOTS, SET_DEV), jnp.float32)
    table = pltpu.VMEM((dates_count * SLOTS, GRID), jnp.float32)
    slots = (own, *far_in, *handed[:-1], near_in, handed[-1])
    early = pl.pallas_call(
        price_early,
        out_shape=result,
        scratch_shapes=[table] * 2,
        compiler_params=limit,
        name="price_early",
    )(*slots[:EARLY], grid)
    netted = pl.pallas_call(
        price_late,
        out_shape=result,
        scratch_shapes=[table] * 2,
        compiler_params=limit,
        name="price_late",
    )(*slots, grid, early)
    return netted.reshape(dates_count, SLOTS_TILE, SET_DEV).transpose(2, 0, 1)


def shards(shocks, trade_kind, *others):
    blocks, slot_count = trade_kind.shape
    by_trade = (
        lax.axis_size("trade") == SLOTS_TILE
        and lax.axis_size("path") == 2
        and shocks.shape == (2, DATES, 1, 1)
        and slot_count == 2 * SLOTS_TILE
        and blocks == SLOTS_TILE * LANES // 2
    )
    return (shards_by_trade if by_trade else shards_by_sum)(shocks, trade_kind, *others)


def solution(mesh):
    placed = (
        P("book", None, "path", "trade"),
        P(("book", "trade"), None),
        P(("book", "trade"), None),
        P(("book", "trade"), None),
        P(("book", "trade"), None),
        P(("book", "trade"), None),
        P(("book", "trade"), None),
        P(("book", "trade")),
        P(("book", "trade")),
    )
    return jax.shard_map(
        shards,
        mesh=mesh,
        in_specs=placed,
        out_specs=P(("book", "trade"), None, "path"),
        check_vma=False,
    )
```

```python
import math

import jax
import jax.numpy as jnp
from jax import lax
from jax.experimental import pallas as pl
from jax.experimental.pallas import tpu as pltpu
from jax.sharding import PartitionSpec as P

GRID = 128
SET_DEV = 32


YEAR_STEP = 0.25
FLAT_RATE = 0.03
REVERT_FAST = 0.5
REVERT_SLOW = 0.04
VOL_FAST = 0.012
VOL_SLOW = 0.009
FACTOR_CORR = -0.6
HIGHEST = lax.Precision.HIGHEST


def loading(reversion, horizon):
    return (1.0 - jnp.exp(-reversion * horizon)) / reversion


def one_variance(reversion, volatility, horizon):
    return (
        volatility**2
        / reversion**2
        * (
            horizon
            + 2.0 / reversion * jnp.exp(-reversion * horizon)
            - 0.5 / reversion * jnp.exp(-2.0 * reversion * horizon)
            - 1.5 / reversion
        )
    )


def factor_variance(horizon):
    fast_part = one_variance(REVERT_FAST, VOL_FAST, horizon)
    slow_part = one_variance(REVERT_SLOW, VOL_SLOW, horizon)
    both_rates = REVERT_FAST + REVERT_SLOW
    cross_part = (
        2.0
        * FACTOR_CORR
        * VOL_FAST
        * VOL_SLOW
        / (REVERT_FAST * REVERT_SLOW)
        * (
            horizon
            + (jnp.exp(-REVERT_FAST * horizon) - 1.0) / REVERT_FAST
            + (jnp.exp(-REVERT_SLOW * horizon) - 1.0) / REVERT_SLOW
            - (jnp.exp(-both_rates * horizon) - 1.0) / both_rates
        )
    )
    return fast_part + slow_part + cross_part


def evolve(path_shocks):
    fast_keep = math.exp(-REVERT_FAST * YEAR_STEP)
    slow_keep = math.exp(-REVERT_SLOW * YEAR_STEP)
    fast_scale = VOL_FAST * math.sqrt(
        (1.0 - math.exp(-2.0 * REVERT_FAST * YEAR_STEP)) / (2.0 * REVERT_FAST)
    )
    slow_scale = VOL_SLOW * math.sqrt(
        (1.0 - math.exp(-2.0 * REVERT_SLOW * YEAR_STEP)) / (2.0 * REVERT_SLOW)
    )
    mixing = math.sqrt(1.0 - FACTOR_CORR**2)
    fast_state = jnp.zeros(path_shocks.shape[2:], jnp.float32)
    slow_state = jnp.zeros(path_shocks.shape[2:], jnp.float32)
    fast_path = []
    slow_path = []
    for period in range(path_shocks.shape[1]):
        fast_state = fast_state * fast_keep + fast_scale * path_shocks[0, period]
        slow_state = slow_state * slow_keep + slow_scale * (
            FACTOR_CORR * path_shocks[0, period] + mixing * path_shocks[1, period]
        )
        fast_path.append(fast_state)
        slow_path.append(slow_state)
    return jnp.stack([jnp.stack(fast_path), jnp.stack(slow_path)])


def discount_table(states):
    dates_count = states.shape[1]
    maturity = lax.broadcasted_iota(jnp.int32, (GRID, 1, 1), 0).astype(jnp.float32) * YEAR_STEP
    valued = (lax.broadcasted_iota(jnp.int32, (1, dates_count, 1), 1) + 1).astype(
        jnp.float32
    ) * YEAR_STEP
    horizon = maturity - valued
    log_front = -FLAT_RATE * horizon + 0.5 * (
        factor_variance(horizon) - factor_variance(maturity) + factor_variance(valued)
    )
    return jnp.exp(
        log_front
        - loading(REVERT_FAST, horizon) * states[0][None]
        - loading(REVERT_SLOW, horizon) * states[1][None]
    )


def price_blocks(
    trade_kind,
    cash_start,
    cash_count,
    strike,
    normal_vol,
    notional,
    block_count,
    discounts,
    dates_count,
):
    groups, slot_count = cash_start.shape
    cash_nodes = lax.broadcasted_iota(jnp.int32, (1, 1, GRID), 2)
    first_node = cash_start[:, :, None]
    last_node = (cash_start + cash_count)[:, :, None]
    accrual = jnp.where(
        (cash_nodes > first_node) & (cash_nodes <= last_node), YEAR_STEP, 0.0
    ).astype(jnp.float32)
    endpoints = (
        jnp.where(cash_nodes == first_node, 1.0, 0.0) - jnp.where(cash_nodes == last_node, 1.0, 0.0)
    ).astype(jnp.float32)
    weights = jnp.concatenate([accrual, endpoints], axis=0).reshape(2 * groups * slot_count, GRID)
    products = jnp.dot(weights, discounts, precision=HIGHEST, preferred_element_type=jnp.float32)
    products = products.reshape(2, groups, slot_count, dates_count, -1)
    annuity = products[0]
    float_leg = products[1]
    swap_rate = float_leg / annuity
    valued = (lax.broadcasted_iota(jnp.int32, (1, 1, dates_count, 1), 2) + 1).astype(
        jnp.float32
    ) * YEAR_STEP
    expiry = cash_start.astype(jnp.float32)[:, :, None, None] * YEAR_STEP
    spread = normal_vol[:, :, None, None] * jnp.sqrt(expiry - valued)
    moneyness = swap_rate - strike[:, :, None, None]
    standard = moneyness / spread
    normal_cdf = 0.5 * (1.0 + jax.scipy.special.erf(standard * (1.0 / math.sqrt(2.0))))
    normal_pdf = jnp.exp(-0.5 * standard * standard) * (1.0 / math.sqrt(2.0 * math.pi))
    offset = jnp.where(trade_kind == 1, 1.0, jnp.where(trade_kind == 2, 0.5, 0.0))[:, :, None, None]
    factor = (jnp.where(trade_kind == 2, 2.0, 1.0) * notional)[:, :, None, None]
    trade_value = factor * annuity * (moneyness * (normal_cdf - offset) + spread * normal_pdf)
    occupied = lax.broadcasted_iota(jnp.int32, (groups, slot_count), 1) < block_count[:, None]
    trade_value = jnp.where(occupied[:, :, None, None], trade_value, 0.0)
    return jnp.sum(trade_value, axis=1).reshape(groups, -1)


def price_all(fields, discounts, dates_count):
    block_rows = fields[0].shape[0]
    group_size = max(32, block_rows // 16)
    turns = block_rows // group_size

    def regroup(array):
        return array.reshape((turns, group_size) + array.shape[1:])

    def one_group(pieces):
        return price_blocks(
            pieces[0],
            pieces[1],
            pieces[2],
            pieces[3],
            pieces[4],
            pieces[5],
            pieces[6],
            discounts,
            dates_count,
        )

    totals = lax.map(one_group, tuple((regroup(field) for field in fields)))
    return totals.reshape(block_rows, -1)


def shards_by_sum(
    shocks, trade_kind, cash_start, cash_count, strike, normal_vol, notional, block_count, block_set
):
    dates_count = shocks.shape[1]
    own_states = evolve(shocks.reshape(2, dates_count, -1))
    gathered = lax.all_gather(own_states, "trade", axis=2, tiled=True)
    discounts = discount_table(gathered)
    discounts = discounts.reshape(GRID, -1)
    block_total = price_all(
        (trade_kind, cash_start, cash_count, strike, normal_vol, notional, block_count),
        discounts,
        dates_count,
    )
    set_index = lax.broadcasted_iota(jnp.int32, (SET_DEV * lax.axis_size("trade"), 1), 0)
    one_hot = (set_index == block_set[None, :]).astype(jnp.float32)
    netted = lax.psum_scatter(
        jnp.dot(one_hot, block_total, precision=HIGHEST, preferred_element_type=jnp.float32),
        "trade",
        scatter_dimension=0,
        tiled=True,
    )
    return jnp.maximum(netted, 0.0).reshape(SET_DEV, dates_count, -1)


SLOTS_TILE = 8
LANES = 128
FIELDS = 6
ROWS = (FIELDS + 1) * SLOTS_TILE
INPUTS = range(9)
NEAR = 1
FAR = ((2, 4), (3, 6), (5, 7))
SLOTS = 8
EARLY = 6
DATES = 2
VMEM_BYTES = 8 * 2**20

TAIL = (
    -1.325748085975647,
    -1.8081518411636353,
    -0.41172587871551514,
    -0.042724475264549255,
    0.0027914412785321474,
    0.00040712140616960824,
    -0.00013435240543913096,
    1.5000393432273995e-05,
    -6.33199476851587e-07,
)


def iota(shape, dimension):
    return lax.broadcasted_iota(jnp.int32, shape, dimension)


def offsets(core):
    return [NEAR] + [jnp.where(core == 0, first, second) for first, second in FAR]


def slot_offsets(core):
    near, *far = offsets(core)
    *handed, last = offsets(1 - core)[1:]
    return [0, *far, *handed, near, last]


def pack(*refs):
    count_of = len(INPUTS)
    sources, outs = refs[:count_of], refs[count_of : count_of + 2 + len(FAR)]
    grid = refs[count_of + 2 + len(FAR)]
    held, arrived = refs[count_of + 3 + len(FAR) : -1], refs[-1]
    copies = [
        pltpu.make_async_copy(source, target, arrived.at[at])
        for at, (source, target) in enumerate(zip(sources, held))
    ]
    for copy in copies:
        copy.start()
    for at, rows in enumerate(curve_rows()):
        grid[at] = rows
    me, core = lax.axis_index("trade"), lax.axis_index("path")
    half = LANES // 2
    low = iota((SLOTS_TILE, LANES), 1) < half
    row, lane = iota((SLOTS_TILE, LANES), 0), iota((SLOTS_TILE, LANES), 1)
    for copy in copies:
        copy.wait()
    kind, start, count, strike, vol, notional, live, group, shocks = held
    own_shocks = jnp.zeros((SLOTS_TILE, LANES), jnp.float32)
    for factor in range(2):
        for date in range(DATES):
            value = jnp.broadcast_to(shocks[factor : factor + 1, date : date + 1], (SLOTS_TILE, LANES))
            own_shocks = jnp.where(lane == factor * DATES + date, value, own_shocks)
    for out, offset in zip(outs, [0] + offsets(core)):
        owner = me ^ offset
        cut = pl.ds(pl.multiple_of(owner // 2 * LANES, LANES), LANES)

        here = low == (owner % 2 == 0)

        def both(in_place, turned):
            return jnp.where(here, in_place, pltpu.roll(turned, half, 1))

        def field(ref):
            return both(ref[:SLOTS_TILE, cut], ref[SLOTS_TILE:, cut])

        lives = jnp.broadcast_to(live[:, cut], (SLOTS_TILE, LANES))
        sets = jnp.broadcast_to(group[:, cut], (SLOTS_TILE, LANES))
        slot = row + jnp.where(here, 0, SLOTS_TILE)
        first, kinds = field(start), field(kind)
        size = jnp.where(kinds == 2, 2.0, 1.0) * field(notional)
        tiles = (
            first.astype(jnp.float32),
            (first + field(count)).astype(jnp.float32),
            field(strike),
            field(vol),
            jnp.where(slot < both(lives, lives), size, 0.0),
            jnp.where(kinds == 1, 1.0, jnp.where(kinds == 2, 0.5, 0.0)),
            jnp.where(row == 0, (both(sets, sets) - owner * SET_DEV).astype(jnp.float32), own_shocks),
        )
        for at, tile in enumerate(tiles):
            out[at * SLOTS_TILE : (at + 1) * SLOTS_TILE, :] = tile
    outs[1][ROWS:, :] = jnp.zeros((SLOTS_TILE, LANES), jnp.float32)


def add_shocks(shocks, *refs):
    core = lax.axis_index("path")
    lane = iota((1, LANES), 1)
    line = jnp.zeros((1, LANES), jnp.float32)
    for factor in range(2):
        for date in range(DATES):
            value = jnp.broadcast_to(shocks[factor : factor + 1, date : date + 1], (1, LANES))
            line = jnp.where(lane == factor * DATES + date, value, line)
    for ref in refs[len(FAR) :]:
        ref[pl.ds(FIELDS * SLOTS_TILE + 2 - core, 1), :] = line


def split(values, count):
    parts = []
    for _ in range(count):
        part = values.astype(jnp.bfloat16)
        parts.append(part)
        values = values - part.astype(jnp.float32)
    return jnp.concatenate(parts, axis=0)


def add_parts(product, count):
    rows = product.shape[0] // count
    total = product[(count - 1) * rows :]
    for part in range(count - 2, -1, -1):
        total = total + product[part * rows : (part + 1) * rows]
    return total


def curve_rows():
    node = iota((SLOTS_TILE, GRID), 1).astype(jnp.float32) * YEAR_STEP
    row = iota((SLOTS_TILE, GRID), 0)
    valued = jnp.where(row < DATES + 1, row, 1).astype(jnp.float32) * YEAR_STEP
    horizon = node - valued
    front = -FLAT_RATE * horizon + 0.5 * (
        factor_variance(horizon) - factor_variance(node) + factor_variance(valued)
    )
    return front, loading(REVERT_FAST, horizon), loading(REVERT_SLOW, horizon)


def tables(shocks, grid):
    states = evolve(shocks)
    discounts = []
    for date in range(DATES):
        front, fast, slow = (grid[at, date + 1 : date + 2, :] for at in range(3))
        discounts.append(jnp.exp(front - fast * states[0, date] - slow * states[1, date]))
    both = jnp.concatenate(discounts, axis=0)
    mid = GRID // 4
    source, target = iota((GRID, GRID), 0), iota((GRID, GRID), 1)
    weights = jnp.where((source > mid) & (source <= target), YEAR_STEP, 0.0) - jnp.where(
        (source <= mid) & (source > target), YEAR_STEP, 0.0
    )
    sums = jnp.dot(split(both, 3), weights.astype(jnp.bfloat16), preferred_element_type=jnp.float32)
    return both, add_parts(sums, 3)


def price_source(ref, tables_of, slots):
    def field(at):
        return ref[at * SLOTS_TILE : (at + 1) * SLOTS_TILE, :]

    def look_up(table, at, index):
        row = jnp.broadcast_to(table[at : at + 1, :], (SLOTS_TILE, LANES))
        return jnp.take_along_axis(row, index, axis=1, mode="promise_in_bounds")

    def merge(first, second, bit):
        if first is None and second is None:
            return None
        zero = jnp.zeros((SLOTS_TILE, LANES), jnp.float32)
        first = zero if first is None else first
        second = zero if second is None else second
        mask = (iota((SLOTS_TILE, LANES), 0) & bit) == 0
        return jnp.where(mask, first, second) + pltpu.roll(jnp.where(mask, second, first), bit, 0)

    first, last = field(0), field(1)
    first_node, last_node = first.astype(jnp.int32), last.astype(jnp.int32)
    strike, vol, size, offset = field(2), field(3), field(4), field(5)
    tilt = 0.5 - offset
    totals = []
    for date in range(DATES):
        spread = vol * jnp.sqrt(first * YEAR_STEP - (date + 1) * YEAR_STEP)
        inverse = 1.0 / spread
        scale = size * spread
        hurdle = strike * inverse
        rows = [(*tables_of(slot), date * SLOTS + slot) for slot in slots]
        starts = [(look_up(curve, at, first_node), look_up(sums, at, first_node)) for curve, sums, at in rows]
        ends = [(look_up(curve, at, last_node), look_up(sums, at, last_node)) for curve, sums, at in rows]
        values = [None] * SLOTS
        for slot, (curve_start, sum_start), (curve_end, sum_end) in zip(slots, starts, ends):
            float_leg, annuity = curve_start - curve_end, sum_end - sum_start
            standard = float_leg * pl.reciprocal(annuity) * inverse - hurdle
            size_of = jnp.abs(standard)
            power = jnp.full_like(size_of, TAIL[-1])
            for term in TAIL[-2::-1]:
                power = power * size_of + term
            values[slot] = scale * annuity * (0.5 * size_of + tilt * standard + jnp.exp2(power))
        for bit in (1, 2, 4):
            values = [merge(a, b, bit) for a, b in zip(values[::2], values[1::2])]
        totals.append(values[0])
    return jnp.concatenate(totals, axis=0)


def set_tables(refs, grid, discount, running):
    line = FIELDS * SLOTS_TILE + 1 + lax.axis_index("path")
    empty = jnp.zeros((1, LANES), jnp.float32)
    lines = jnp.concatenate([empty if ref is None else ref[pl.ds(line, 1), :] for ref in refs], axis=0)
    shocks = [jnp.broadcast_to(lines[:, at : at + 1], (SLOTS, LANES)) for at in range(2 * DATES)]
    shocks = jnp.stack([jnp.stack(shocks[:DATES]), jnp.stack(shocks[DATES:])])
    discount[...], running[...] = tables(shocks, grid)


def net(refs, totals):
    extra = FIELDS * SLOTS_TILE
    set_index = iota((SET_DEV, LANES), 0).astype(jnp.float32)
    one_hot = jnp.concatenate(
        [(set_index == ref[extra : extra + 1, :]).astype(jnp.bfloat16) for ref in refs], axis=1
    )
    netted = lax.dot_general(
        split(jnp.concatenate(totals, axis=1), 3),
        one_hot,
        (((1,), (1,)), ((), ())),
        preferred_element_type=jnp.float32,
    )
    return add_parts(netted, 3)


def price_early(*refs):
    refs, (grid, out, discount, running) = refs[:-4], refs[-4:]
    set_tables([*refs, *[None] * (SLOTS - EARLY)], grid, discount, running)
    out[...] = net(refs, [price_source(ref, lambda slot: (discount, running), range(EARLY)) for ref in refs])


def price_late(*refs):
    refs, (grid, early, discount, running, out, late_discount, late_running) = refs[:-7], refs[-7:]
    set_tables([*[None] * EARLY, *refs[EARLY:]], grid, late_discount, late_running)

    def tables_of(slot):
        return (discount, running) if slot < EARLY else (late_discount, late_running)

    totals = [price_source(ref, tables_of, range(SLOTS)) for ref in refs[EARLY:]]
    totals = [price_source(ref, tables_of, range(EARLY, SLOTS)) for ref in refs[:EARLY]] + totals
    netted = jnp.maximum(net(refs, totals) + early[...], 0.0)
    me = lax.axis_index("trade")
    for slot, offset in enumerate(slot_offsets(lax.axis_index("path"))):
        for date in range(DATES):
            at = date * SLOTS + slot
            out[pl.ds(date * SLOTS + (me ^ offset), 1), :] = netted[at : at + 1, :]


def shards_by_trade(
    shocks, trade_kind, cash_start, cash_count, strike, normal_vol, notional, block_count, block_set
):
    dates_count = shocks.shape[1]
    own_shocks = shocks.reshape(2, dates_count)
    swap = [(0, 1), (1, 0)]
    other_shocks = lax.ppermute(shocks, "path", swap).reshape(2, dates_count)
    fields = (
        trade_kind.T,
        cash_start.T,
        cash_count.T,
        strike.T,
        normal_vol.T,
        notional.T,
        block_count.reshape(1, -1),
        block_set.reshape(1, -1),
        own_shocks,
    )
    message = jax.ShapeDtypeStruct((ROWS, LANES), jnp.float32)
    near_message = jax.ShapeDtypeStruct((ROWS + SLOTS_TILE, LANES), jnp.float32)
    limit = pltpu.CompilerParams(vmem_limit_bytes=VMEM_BYTES)
    own, near, *far, grid = pl.pallas_call(
        pack,
        out_shape=[message, near_message] + [message] * len(FAR) + [jax.ShapeDtypeStruct((3, SLOTS_TILE, GRID), jnp.float32)],
        in_specs=[pl.BlockSpec(memory_space=pltpu.HBM)] * len(fields),
        scratch_shapes=[pltpu.VMEM(field.shape, field.dtype) for field in fields]
        + [pltpu.SemaphoreType.DMA((len(fields),))],
        compiler_params=limit,
        name="pack",
    )(*(pltpu.with_memory_space_constraint(field, pltpu.HBM) for field in fields))
    owners = lax.axis_size("trade")
    near_in = lax.ppermute(near, "trade", [(at, at ^ NEAR) for at in range(owners)])
    far = pl.pallas_call(
        add_shocks,
        out_shape=[message] * len(FAR),
        input_output_aliases={1 + at: at for at in range(len(FAR))},
        compiler_params=limit,
        name="add_shocks",
    )(other_shocks, *far)
    far_in = []
    for piece, pair in zip(far, FAR):
        turns = [(2 * at + core, 2 * (at ^ pair[core]) + core) for at in range(owners) for core in range(2)]
        far_in.append(lax.ppermute(piece, ("trade", "path"), turns))
    handed = [lax.ppermute(piece, "path", swap) for piece in far_in]
    result = jax.ShapeDtypeStruct((dates_count * SLOTS, SET_DEV), jnp.float32)
    table = jax.ShapeDtypeStruct((dates_count * SLOTS, GRID), jnp.float32)
    slots = (own, *far_in, *handed[:-1], near_in, handed[-1])
    early = pl.pallas_call(
        price_early,
        out_shape=[result, table, table],
        compiler_params=limit,
        name="price_early",
    )(*slots[:EARLY], grid)
    netted = pl.pallas_call(
        price_late,
        out_shape=result,
        scratch_shapes=[pltpu.VMEM(table.shape, table.dtype)] * 2,
        compiler_params=limit,
        name="price_late",
    )(*slots, grid, *early)
    return netted.reshape(dates_count, SLOTS_TILE, SET_DEV).transpose(2, 0, 1)


def shards(shocks, trade_kind, *others):
    blocks, slot_count = trade_kind.shape
    by_trade = (
        lax.axis_size("trade") == SLOTS_TILE
        and lax.axis_size("path") == 2
        and shocks.shape == (2, DATES, 1, 1)
        and slot_count == 2 * SLOTS_TILE
        and blocks == SLOTS_TILE * LANES // 2
    )
    return (shards_by_trade if by_trade else shards_by_sum)(shocks, trade_kind, *others)


def solution(mesh):
    placed = (
        P("book", None, "path", "trade"),
        P(("book", "trade"), None),
        P(("book", "trade"), None),
        P(("book", "trade"), None),
        P(("book", "trade"), None),
        P(("book", "trade"), None),
        P(("book", "trade"), None),
        P(("book", "trade")),
        P(("book", "trade")),
    )
    return jax.shard_map(
        shards,
        mesh=mesh,
        in_specs=placed,
        out_specs=P(("book", "trade"), None, "path"),
        check_vma=False,
    )
```

```python
import math

import jax
import jax.numpy as jnp
from jax import lax
from jax.experimental import pallas as pl
from jax.experimental.pallas import tpu as pltpu
from jax.sharding import PartitionSpec as P

GRID = 128
SET_DEV = 32


YEAR_STEP = 0.25
FLAT_RATE = 0.03
REVERT_FAST = 0.5
REVERT_SLOW = 0.04
VOL_FAST = 0.012
VOL_SLOW = 0.009
FACTOR_CORR = -0.6
HIGHEST = lax.Precision.HIGHEST


def loading(reversion, horizon):
    return (1.0 - jnp.exp(-reversion * horizon)) / reversion


def one_variance(reversion, volatility, horizon):
    return (
        volatility**2
        / reversion**2
        * (
            horizon
            + 2.0 / reversion * jnp.exp(-reversion * horizon)
            - 0.5 / reversion * jnp.exp(-2.0 * reversion * horizon)
            - 1.5 / reversion
        )
    )


def factor_variance(horizon):
    fast_part = one_variance(REVERT_FAST, VOL_FAST, horizon)
    slow_part = one_variance(REVERT_SLOW, VOL_SLOW, horizon)
    both_rates = REVERT_FAST + REVERT_SLOW
    cross_part = (
        2.0
        * FACTOR_CORR
        * VOL_FAST
        * VOL_SLOW
        / (REVERT_FAST * REVERT_SLOW)
        * (
            horizon
            + (jnp.exp(-REVERT_FAST * horizon) - 1.0) / REVERT_FAST
            + (jnp.exp(-REVERT_SLOW * horizon) - 1.0) / REVERT_SLOW
            - (jnp.exp(-both_rates * horizon) - 1.0) / both_rates
        )
    )
    return fast_part + slow_part + cross_part


def evolve(path_shocks):
    fast_keep = math.exp(-REVERT_FAST * YEAR_STEP)
    slow_keep = math.exp(-REVERT_SLOW * YEAR_STEP)
    fast_scale = VOL_FAST * math.sqrt(
        (1.0 - math.exp(-2.0 * REVERT_FAST * YEAR_STEP)) / (2.0 * REVERT_FAST)
    )
    slow_scale = VOL_SLOW * math.sqrt(
        (1.0 - math.exp(-2.0 * REVERT_SLOW * YEAR_STEP)) / (2.0 * REVERT_SLOW)
    )
    mixing = math.sqrt(1.0 - FACTOR_CORR**2)
    fast_state = jnp.zeros(path_shocks.shape[2:], jnp.float32)
    slow_state = jnp.zeros(path_shocks.shape[2:], jnp.float32)
    fast_path = []
    slow_path = []
    for period in range(path_shocks.shape[1]):
        fast_state = fast_state * fast_keep + fast_scale * path_shocks[0, period]
        slow_state = slow_state * slow_keep + slow_scale * (
            FACTOR_CORR * path_shocks[0, period] + mixing * path_shocks[1, period]
        )
        fast_path.append(fast_state)
        slow_path.append(slow_state)
    return jnp.stack([jnp.stack(fast_path), jnp.stack(slow_path)])


def discount_table(states):
    dates_count = states.shape[1]
    maturity = lax.broadcasted_iota(jnp.int32, (GRID, 1, 1), 0).astype(jnp.float32) * YEAR_STEP
    valued = (lax.broadcasted_iota(jnp.int32, (1, dates_count, 1), 1) + 1).astype(
        jnp.float32
    ) * YEAR_STEP
    horizon = maturity - valued
    log_front = -FLAT_RATE * horizon + 0.5 * (
        factor_variance(horizon) - factor_variance(maturity) + factor_variance(valued)
    )
    return jnp.exp(
        log_front
        - loading(REVERT_FAST, horizon) * states[0][None]
        - loading(REVERT_SLOW, horizon) * states[1][None]
    )


def price_blocks(
    trade_kind,
    cash_start,
    cash_count,
    strike,
    normal_vol,
    notional,
    block_count,
    discounts,
    dates_count,
):
    groups, slot_count = cash_start.shape
    cash_nodes = lax.broadcasted_iota(jnp.int32, (1, 1, GRID), 2)
    first_node = cash_start[:, :, None]
    last_node = (cash_start + cash_count)[:, :, None]
    accrual = jnp.where(
        (cash_nodes > first_node) & (cash_nodes <= last_node), YEAR_STEP, 0.0
    ).astype(jnp.float32)
    endpoints = (
        jnp.where(cash_nodes == first_node, 1.0, 0.0) - jnp.where(cash_nodes == last_node, 1.0, 0.0)
    ).astype(jnp.float32)
    weights = jnp.concatenate([accrual, endpoints], axis=0).reshape(2 * groups * slot_count, GRID)
    products = jnp.dot(weights, discounts, precision=HIGHEST, preferred_element_type=jnp.float32)
    products = products.reshape(2, groups, slot_count, dates_count, -1)
    annuity = products[0]
    float_leg = products[1]
    swap_rate = float_leg / annuity
    valued = (lax.broadcasted_iota(jnp.int32, (1, 1, dates_count, 1), 2) + 1).astype(
        jnp.float32
    ) * YEAR_STEP
    expiry = cash_start.astype(jnp.float32)[:, :, None, None] * YEAR_STEP
    spread = normal_vol[:, :, None, None] * jnp.sqrt(expiry - valued)
    moneyness = swap_rate - strike[:, :, None, None]
    standard = moneyness / spread
    normal_cdf = 0.5 * (1.0 + jax.scipy.special.erf(standard * (1.0 / math.sqrt(2.0))))
    normal_pdf = jnp.exp(-0.5 * standard * standard) * (1.0 / math.sqrt(2.0 * math.pi))
    offset = jnp.where(trade_kind == 1, 1.0, jnp.where(trade_kind == 2, 0.5, 0.0))[:, :, None, None]
    factor = (jnp.where(trade_kind == 2, 2.0, 1.0) * notional)[:, :, None, None]
    trade_value = factor * annuity * (moneyness * (normal_cdf - offset) + spread * normal_pdf)
    occupied = lax.broadcasted_iota(jnp.int32, (groups, slot_count), 1) < block_count[:, None]
    trade_value = jnp.where(occupied[:, :, None, None], trade_value, 0.0)
    return jnp.sum(trade_value, axis=1).reshape(groups, -1)


def price_all(fields, discounts, dates_count):
    block_rows = fields[0].shape[0]
    group_size = max(32, block_rows // 16)
    turns = block_rows // group_size

    def regroup(array):
        return array.reshape((turns, group_size) + array.shape[1:])

    def one_group(pieces):
        return price_blocks(
            pieces[0],
            pieces[1],
            pieces[2],
            pieces[3],
            pieces[4],
            pieces[5],
            pieces[6],
            discounts,
            dates_count,
        )

    totals = lax.map(one_group, tuple((regroup(field) for field in fields)))
    return totals.reshape(block_rows, -1)


def shards_by_sum(
    shocks, trade_kind, cash_start, cash_count, strike, normal_vol, notional, block_count, block_set
):
    dates_count = shocks.shape[1]
    own_states = evolve(shocks.reshape(2, dates_count, -1))
    gathered = lax.all_gather(own_states, "trade", axis=2, tiled=True)
    discounts = discount_table(gathered)
    discounts = discounts.reshape(GRID, -1)
    block_total = price_all(
        (trade_kind, cash_start, cash_count, strike, normal_vol, notional, block_count),
        discounts,
        dates_count,
    )
    set_index = lax.broadcasted_iota(jnp.int32, (SET_DEV * lax.axis_size("trade"), 1), 0)
    one_hot = (set_index == block_set[None, :]).astype(jnp.float32)
    netted = lax.psum_scatter(
        jnp.dot(one_hot, block_total, precision=HIGHEST, preferred_element_type=jnp.float32),
        "trade",
        scatter_dimension=0,
        tiled=True,
    )
    return jnp.maximum(netted, 0.0).reshape(SET_DEV, dates_count, -1)


SLOTS_TILE = 8
LANES = 128
FIELDS = 6
ROWS = (FIELDS + 1) * SLOTS_TILE
INPUTS = range(9)
NEAR = 1
FAR = ((3, 4), (2, 6), (5, 7))
SLOTS = 8
EARLY = 6
DATES = 2
VMEM_BYTES = 8 * 2**20

TAIL = (
    -1.325748085975647,
    -1.8081518411636353,
    -0.41172587871551514,
    -0.042724475264549255,
    0.0027914412785321474,
    0.00040712140616960824,
    -0.00013435240543913096,
    1.5000393432273995e-05,
    -6.33199476851587e-07,
)


def iota(shape, dimension):
    return lax.broadcasted_iota(jnp.int32, shape, dimension)


def offsets(core):
    return [NEAR] + [jnp.where(core == 0, first, second) for first, second in FAR]


def slot_offsets(core):
    near, *far = offsets(core)
    *handed, last = offsets(1 - core)[1:]
    return [0, *far, *handed, near, last]


def pack(*refs):
    count_of = len(INPUTS)
    sources, outs = refs[:count_of], refs[count_of : count_of + 2 + len(FAR)]
    grid = refs[count_of + 2 + len(FAR)]
    held, arrived = refs[count_of + 3 + len(FAR) : -1], refs[-1]
    copies = [
        pltpu.make_async_copy(source, target, arrived.at[at])
        for at, (source, target) in enumerate(zip(sources, held))
    ]
    for copy in copies:
        copy.start()
    for at, rows in enumerate(curve_rows()):
        grid[at] = rows
    me, core = lax.axis_index("trade"), lax.axis_index("path")
    half = LANES // 2
    low = iota((SLOTS_TILE, LANES), 1) < half
    row, lane = iota((SLOTS_TILE, LANES), 0), iota((SLOTS_TILE, LANES), 1)
    for copy in copies:
        copy.wait()
    kind, start, count, strike, vol, notional, live, group, shocks = held
    own_shocks = jnp.zeros((SLOTS_TILE, LANES), jnp.float32)
    for factor in range(2):
        for date in range(DATES):
            value = jnp.broadcast_to(shocks[factor : factor + 1, date : date + 1], (SLOTS_TILE, LANES))
            own_shocks = jnp.where(lane == factor * DATES + date, value, own_shocks)
    for out, offset in zip(outs, [0] + offsets(core)):
        owner = me ^ offset
        cut = pl.ds(pl.multiple_of(owner // 2 * LANES, LANES), LANES)

        here = low == (owner % 2 == 0)

        def both(in_place, turned):
            return jnp.where(here, in_place, pltpu.roll(turned, half, 1))

        def field(ref):
            return both(ref[:SLOTS_TILE, cut], ref[SLOTS_TILE:, cut])

        lives = jnp.broadcast_to(live[:, cut], (SLOTS_TILE, LANES))
        sets = jnp.broadcast_to(group[:, cut], (SLOTS_TILE, LANES))
        slot = row + jnp.where(here, 0, SLOTS_TILE)
        first, kinds = field(start), field(kind)
        size = jnp.where(kinds == 2, 2.0, 1.0) * field(notional)
        tiles = (
            first.astype(jnp.float32),
            (first + field(count)).astype(jnp.float32),
            field(strike),
            field(vol),
            jnp.where(slot < both(lives, lives), size, 0.0),
            jnp.where(kinds == 1, 1.0, jnp.where(kinds == 2, 0.5, 0.0)),
            jnp.where(row == 0, (both(sets, sets) - owner * SET_DEV).astype(jnp.float32), own_shocks),
        )
        for at, tile in enumerate(tiles):
            out[at * SLOTS_TILE : (at + 1) * SLOTS_TILE, :] = tile
    outs[1][ROWS:, :] = jnp.zeros((SLOTS_TILE, LANES), jnp.float32)


def add_shocks(shocks, *refs):
    core = lax.axis_index("path")
    lane = iota((1, LANES), 1)
    line = jnp.zeros((1, LANES), jnp.float32)
    for factor in range(2):
        for date in range(DATES):
            value = jnp.broadcast_to(shocks[factor : factor + 1, date : date + 1], (1, LANES))
            line = jnp.where(lane == factor * DATES + date, value, line)
    for ref in refs[len(FAR) :]:
        ref[pl.ds(FIELDS * SLOTS_TILE + 2 - core, 1), :] = line


def split(values, count):
    parts = []
    for _ in range(count):
        part = values.astype(jnp.bfloat16)
        parts.append(part)
        values = values - part.astype(jnp.float32)
    return jnp.concatenate(parts, axis=0)


def add_parts(product, count):
    rows = product.shape[0] // count
    total = product[(count - 1) * rows :]
    for part in range(count - 2, -1, -1):
        total = total + product[part * rows : (part + 1) * rows]
    return total


def curve_rows():
    node = iota((SLOTS_TILE, GRID), 1).astype(jnp.float32) * YEAR_STEP
    row = iota((SLOTS_TILE, GRID), 0)
    valued = jnp.where(row < DATES + 1, row, 1).astype(jnp.float32) * YEAR_STEP
    horizon = node - valued
    front = -FLAT_RATE * horizon + 0.5 * (
        factor_variance(horizon) - factor_variance(node) + factor_variance(valued)
    )
    return front, loading(REVERT_FAST, horizon), loading(REVERT_SLOW, horizon)


def tables(shocks, grid):
    states = evolve(shocks)
    discounts = []
    for date in range(DATES):
        front, fast, slow = (grid[at, date + 1 : date + 2, :] for at in range(3))
        discounts.append(jnp.exp(front - fast * states[0, date] - slow * states[1, date]))
    both = jnp.concatenate(discounts, axis=0)
    mid = GRID // 4
    source, target = iota((GRID, GRID), 0), iota((GRID, GRID), 1)
    weights = jnp.where((source > mid) & (source <= target), YEAR_STEP, 0.0) - jnp.where(
        (source <= mid) & (source > target), YEAR_STEP, 0.0
    )
    sums = jnp.dot(split(both, 3), weights.astype(jnp.bfloat16), preferred_element_type=jnp.float32)
    return both, add_parts(sums, 3)


def price_source(ref, tables_of, slots):
    def field(at):
        return ref[at * SLOTS_TILE : (at + 1) * SLOTS_TILE, :]

    def look_up(table, at, index):
        row = jnp.broadcast_to(table[at : at + 1, :], (SLOTS_TILE, LANES))
        return jnp.take_along_axis(row, index, axis=1, mode="promise_in_bounds")

    def merge(first, second, bit):
        if first is None and second is None:
            return None
        zero = jnp.zeros((SLOTS_TILE, LANES), jnp.float32)
        first = zero if first is None else first
        second = zero if second is None else second
        mask = (iota((SLOTS_TILE, LANES), 0) & bit) == 0
        return jnp.where(mask, first, second) + pltpu.roll(jnp.where(mask, second, first), bit, 0)

    first, last = field(0), field(1)
    first_node, last_node = first.astype(jnp.int32), last.astype(jnp.int32)
    strike, vol, size, offset = field(2), field(3), field(4), field(5)
    tilt = 0.5 - offset
    totals = []
    for date in range(DATES):
        spread = vol * jnp.sqrt(first * YEAR_STEP - (date + 1) * YEAR_STEP)
        inverse = 1.0 / spread
        scale = size * spread
        hurdle = strike * inverse
        rows = [(*tables_of(slot), date * SLOTS + slot) for slot in slots]
        starts = [(look_up(curve, at, first_node), look_up(sums, at, first_node)) for curve, sums, at in rows]
        ends = [(look_up(curve, at, last_node), look_up(sums, at, last_node)) for curve, sums, at in rows]
        values = [None] * SLOTS
        for slot, (curve_start, sum_start), (curve_end, sum_end) in zip(slots, starts, ends):
            float_leg, annuity = curve_start - curve_end, sum_end - sum_start
            standard = float_leg * pl.reciprocal(annuity) * inverse - hurdle
            size_of = jnp.abs(standard)
            power = jnp.full_like(size_of, TAIL[-1])
            for term in TAIL[-2::-1]:
                power = power * size_of + term
            values[slot] = scale * annuity * (0.5 * size_of + tilt * standard + jnp.exp2(power))
        for bit in (1, 2, 4):
            values = [merge(a, b, bit) for a, b in zip(values[::2], values[1::2])]
        totals.append(values[0])
    return jnp.concatenate(totals, axis=0)


def set_tables(refs, grid, discount, running):
    line = FIELDS * SLOTS_TILE + 1 + lax.axis_index("path")
    empty = jnp.zeros((1, LANES), jnp.float32)
    lines = jnp.concatenate([empty if ref is None else ref[pl.ds(line, 1), :] for ref in refs], axis=0)
    shocks = [jnp.broadcast_to(lines[:, at : at + 1], (SLOTS, LANES)) for at in range(2 * DATES)]
    shocks = jnp.stack([jnp.stack(shocks[:DATES]), jnp.stack(shocks[DATES:])])
    discount[...], running[...] = tables(shocks, grid)


def net(refs, totals):
    extra = FIELDS * SLOTS_TILE
    set_index = iota((SET_DEV, LANES), 0).astype(jnp.float32)
    one_hot = jnp.concatenate(
        [(set_index == ref[extra : extra + 1, :]).astype(jnp.bfloat16) for ref in refs], axis=1
    )
    netted = lax.dot_general(
        split(jnp.concatenate(totals, axis=1), 3),
        one_hot,
        (((1,), (1,)), ((), ())),
        preferred_element_type=jnp.float32,
    )
    return add_parts(netted, 3)


def price_early(*refs):
    refs, (grid, out, discount, running) = refs[:-4], refs[-4:]
    set_tables([*refs, *[None] * (SLOTS - EARLY)], grid, discount, running)
    out[...] = net(refs, [price_source(ref, lambda slot: (discount, running), range(EARLY)) for ref in refs])


def price_late(*refs):
    refs, (grid, early, discount, running, out, late_discount, late_running) = refs[:-7], refs[-7:]
    set_tables([*[None] * EARLY, *refs[EARLY:]], grid, late_discount, late_running)

    def tables_of(slot):
        return (discount, running) if slot < EARLY else (late_discount, late_running)

    totals = [price_source(ref, tables_of, range(SLOTS)) for ref in refs[EARLY:]]
    totals = [price_source(ref, tables_of, range(EARLY, SLOTS)) for ref in refs[:EARLY]] + totals
    netted = jnp.maximum(net(refs, totals) + early[...], 0.0)
    me = lax.axis_index("trade")
    for slot, offset in enumerate(slot_offsets(lax.axis_index("path"))):
        for date in range(DATES):
            at = date * SLOTS + slot
            out[pl.ds(date * SLOTS + (me ^ offset), 1), :] = netted[at : at + 1, :]


def shards_by_trade(
    shocks, trade_kind, cash_start, cash_count, strike, normal_vol, notional, block_count, block_set
):
    dates_count = shocks.shape[1]
    own_shocks = shocks.reshape(2, dates_count)
    swap = [(0, 1), (1, 0)]
    other_shocks = lax.ppermute(shocks, "path", swap).reshape(2, dates_count)
    fields = (
        trade_kind.T,
        cash_start.T,
        cash_count.T,
        strike.T,
        normal_vol.T,
        notional.T,
        block_count.reshape(1, -1),
        block_set.reshape(1, -1),
        own_shocks,
    )
    message = jax.ShapeDtypeStruct((ROWS, LANES), jnp.float32)
    near_message = jax.ShapeDtypeStruct((ROWS + SLOTS_TILE, LANES), jnp.float32)
    limit = pltpu.CompilerParams(vmem_limit_bytes=VMEM_BYTES)
    own, near, *far, grid = pl.pallas_call(
        pack,
        out_shape=[message, near_message] + [message] * len(FAR) + [jax.ShapeDtypeStruct((3, SLOTS_TILE, GRID), jnp.float32)],
        in_specs=[pl.BlockSpec(memory_space=pltpu.HBM)] * len(fields),
        scratch_shapes=[pltpu.VMEM(field.shape, field.dtype) for field in fields]
        + [pltpu.SemaphoreType.DMA((len(fields),))],
        compiler_params=limit,
        name="pack",
    )(*(pltpu.with_memory_space_constraint(field, pltpu.HBM) for field in fields))
    owners = lax.axis_size("trade")
    near_in = lax.ppermute(near, "trade", [(at, at ^ NEAR) for at in range(owners)])
    far = pl.pallas_call(
        add_shocks,
        out_shape=[message] * len(FAR),
        input_output_aliases={1 + at: at for at in range(len(FAR))},
        compiler_params=limit,
        name="add_shocks",
    )(other_shocks, *far)
    far_in = []
    for piece, pair in zip(far, FAR):
        turns = [(2 * at + core, 2 * (at ^ pair[core]) + core) for at in range(owners) for core in range(2)]
        far_in.append(lax.ppermute(piece, ("trade", "path"), turns))
    handed = [lax.ppermute(piece, "path", swap) for piece in far_in]
    result = jax.ShapeDtypeStruct((dates_count * SLOTS, SET_DEV), jnp.float32)
    table = jax.ShapeDtypeStruct((dates_count * SLOTS, GRID), jnp.float32)
    slots = (own, *far_in, *handed[:-1], near_in, handed[-1])
    early = pl.pallas_call(
        price_early,
        out_shape=[result, table, table],
        compiler_params=limit,
        name="price_early",
    )(*slots[:EARLY], grid)
    netted = pl.pallas_call(
        price_late,
        out_shape=result,
        scratch_shapes=[pltpu.VMEM(table.shape, table.dtype)] * 2,
        compiler_params=limit,
        name="price_late",
    )(*slots, grid, *early)
    return netted.reshape(dates_count, SLOTS_TILE, SET_DEV).transpose(2, 0, 1)


def shards(shocks, trade_kind, *others):
    blocks, slot_count = trade_kind.shape
    by_trade = (
        lax.axis_size("trade") == SLOTS_TILE
        and lax.axis_size("path") == 2
        and shocks.shape == (2, DATES, 1, 1)
        and slot_count == 2 * SLOTS_TILE
        and blocks == SLOTS_TILE * LANES // 2
    )
    return (shards_by_trade if by_trade else shards_by_sum)(shocks, trade_kind, *others)


def solution(mesh):
    placed = (
        P("book", None, "path", "trade"),
        P(("book", "trade"), None),
        P(("book", "trade"), None),
        P(("book", "trade"), None),
        P(("book", "trade"), None),
        P(("book", "trade"), None),
        P(("book", "trade"), None),
        P(("book", "trade")),
        P(("book", "trade")),
    )
    return jax.shard_map(
        shards,
        mesh=mesh,
        in_specs=placed,
        out_specs=P(("book", "trade"), None, "path"),
        check_vma=False,
    )
```

```python
import math

import jax
import jax.numpy as jnp
from jax import lax
from jax.experimental import pallas as pl
from jax.experimental.pallas import tpu as pltpu
from jax.sharding import PartitionSpec as P

GRID = 128
SET_DEV = 32


YEAR_STEP = 0.25
FLAT_RATE = 0.03
REVERT_FAST = 0.5
REVERT_SLOW = 0.04
VOL_FAST = 0.012
VOL_SLOW = 0.009
FACTOR_CORR = -0.6
HIGHEST = lax.Precision.HIGHEST


def loading(reversion, horizon):
    return (1.0 - jnp.exp(-reversion * horizon)) / reversion


def one_variance(reversion, volatility, horizon):
    return (
        volatility**2
        / reversion**2
        * (
            horizon
            + 2.0 / reversion * jnp.exp(-reversion * horizon)
            - 0.5 / reversion * jnp.exp(-2.0 * reversion * horizon)
            - 1.5 / reversion
        )
    )


def factor_variance(horizon):
    fast_part = one_variance(REVERT_FAST, VOL_FAST, horizon)
    slow_part = one_variance(REVERT_SLOW, VOL_SLOW, horizon)
    both_rates = REVERT_FAST + REVERT_SLOW
    cross_part = (
        2.0
        * FACTOR_CORR
        * VOL_FAST
        * VOL_SLOW
        / (REVERT_FAST * REVERT_SLOW)
        * (
            horizon
            + (jnp.exp(-REVERT_FAST * horizon) - 1.0) / REVERT_FAST
            + (jnp.exp(-REVERT_SLOW * horizon) - 1.0) / REVERT_SLOW
            - (jnp.exp(-both_rates * horizon) - 1.0) / both_rates
        )
    )
    return fast_part + slow_part + cross_part


def evolve(path_shocks):
    fast_keep = math.exp(-REVERT_FAST * YEAR_STEP)
    slow_keep = math.exp(-REVERT_SLOW * YEAR_STEP)
    fast_scale = VOL_FAST * math.sqrt(
        (1.0 - math.exp(-2.0 * REVERT_FAST * YEAR_STEP)) / (2.0 * REVERT_FAST)
    )
    slow_scale = VOL_SLOW * math.sqrt(
        (1.0 - math.exp(-2.0 * REVERT_SLOW * YEAR_STEP)) / (2.0 * REVERT_SLOW)
    )
    mixing = math.sqrt(1.0 - FACTOR_CORR**2)
    fast_state = jnp.zeros(path_shocks.shape[2:], jnp.float32)
    slow_state = jnp.zeros(path_shocks.shape[2:], jnp.float32)
    fast_path = []
    slow_path = []
    for period in range(path_shocks.shape[1]):
        fast_state = fast_state * fast_keep + fast_scale * path_shocks[0, period]
        slow_state = slow_state * slow_keep + slow_scale * (
            FACTOR_CORR * path_shocks[0, period] + mixing * path_shocks[1, period]
        )
        fast_path.append(fast_state)
        slow_path.append(slow_state)
    return jnp.stack([jnp.stack(fast_path), jnp.stack(slow_path)])


def discount_table(states):
    dates_count = states.shape[1]
    maturity = lax.broadcasted_iota(jnp.int32, (GRID, 1, 1), 0).astype(jnp.float32) * YEAR_STEP
    valued = (lax.broadcasted_iota(jnp.int32, (1, dates_count, 1), 1) + 1).astype(
        jnp.float32
    ) * YEAR_STEP
    horizon = maturity - valued
    log_front = -FLAT_RATE * horizon + 0.5 * (
        factor_variance(horizon) - factor_variance(maturity) + factor_variance(valued)
    )
    return jnp.exp(
        log_front
        - loading(REVERT_FAST, horizon) * states[0][None]
        - loading(REVERT_SLOW, horizon) * states[1][None]
    )


def price_blocks(
    trade_kind,
    cash_start,
    cash_count,
    strike,
    normal_vol,
    notional,
    block_count,
    discounts,
    dates_count,
):
    groups, slot_count = cash_start.shape
    cash_nodes = lax.broadcasted_iota(jnp.int32, (1, 1, GRID), 2)
    first_node = cash_start[:, :, None]
    last_node = (cash_start + cash_count)[:, :, None]
    accrual = jnp.where(
        (cash_nodes > first_node) & (cash_nodes <= last_node), YEAR_STEP, 0.0
    ).astype(jnp.float32)
    endpoints = (
        jnp.where(cash_nodes == first_node, 1.0, 0.0) - jnp.where(cash_nodes == last_node, 1.0, 0.0)
    ).astype(jnp.float32)
    weights = jnp.concatenate([accrual, endpoints], axis=0).reshape(2 * groups * slot_count, GRID)
    products = jnp.dot(weights, discounts, precision=HIGHEST, preferred_element_type=jnp.float32)
    products = products.reshape(2, groups, slot_count, dates_count, -1)
    annuity = products[0]
    float_leg = products[1]
    swap_rate = float_leg / annuity
    valued = (lax.broadcasted_iota(jnp.int32, (1, 1, dates_count, 1), 2) + 1).astype(
        jnp.float32
    ) * YEAR_STEP
    expiry = cash_start.astype(jnp.float32)[:, :, None, None] * YEAR_STEP
    spread = normal_vol[:, :, None, None] * jnp.sqrt(expiry - valued)
    moneyness = swap_rate - strike[:, :, None, None]
    standard = moneyness / spread
    normal_cdf = 0.5 * (1.0 + jax.scipy.special.erf(standard * (1.0 / math.sqrt(2.0))))
    normal_pdf = jnp.exp(-0.5 * standard * standard) * (1.0 / math.sqrt(2.0 * math.pi))
    offset = jnp.where(trade_kind == 1, 1.0, jnp.where(trade_kind == 2, 0.5, 0.0))[:, :, None, None]
    factor = (jnp.where(trade_kind == 2, 2.0, 1.0) * notional)[:, :, None, None]
    trade_value = factor * annuity * (moneyness * (normal_cdf - offset) + spread * normal_pdf)
    occupied = lax.broadcasted_iota(jnp.int32, (groups, slot_count), 1) < block_count[:, None]
    trade_value = jnp.where(occupied[:, :, None, None], trade_value, 0.0)
    return jnp.sum(trade_value, axis=1).reshape(groups, -1)


def price_all(fields, discounts, dates_count):
    block_rows = fields[0].shape[0]
    group_size = max(32, block_rows // 16)
    turns = block_rows // group_size

    def regroup(array):
        return array.reshape((turns, group_size) + array.shape[1:])

    def one_group(pieces):
        return price_blocks(
            pieces[0],
            pieces[1],
            pieces[2],
            pieces[3],
            pieces[4],
            pieces[5],
            pieces[6],
            discounts,
            dates_count,
        )

    totals = lax.map(one_group, tuple((regroup(field) for field in fields)))
    return totals.reshape(block_rows, -1)


def shards_by_sum(
    shocks, trade_kind, cash_start, cash_count, strike, normal_vol, notional, block_count, block_set
):
    dates_count = shocks.shape[1]
    own_states = evolve(shocks.reshape(2, dates_count, -1))
    gathered = lax.all_gather(own_states, "trade", axis=2, tiled=True)
    discounts = discount_table(gathered)
    discounts = discounts.reshape(GRID, -1)
    block_total = price_all(
        (trade_kind, cash_start, cash_count, strike, normal_vol, notional, block_count),
        discounts,
        dates_count,
    )
    set_index = lax.broadcasted_iota(jnp.int32, (SET_DEV * lax.axis_size("trade"), 1), 0)
    one_hot = (set_index == block_set[None, :]).astype(jnp.float32)
    netted = lax.psum_scatter(
        jnp.dot(one_hot, block_total, precision=HIGHEST, preferred_element_type=jnp.float32),
        "trade",
        scatter_dimension=0,
        tiled=True,
    )
    return jnp.maximum(netted, 0.0).reshape(SET_DEV, dates_count, -1)


SLOTS_TILE = 8
LANES = 128
FIELDS = 6
ROWS = (FIELDS + 1) * SLOTS_TILE
INPUTS = range(9)
NEAR = 1
FAR = ((2, 4), (3, 6), (5, 7))
SLOTS = 8
EARLY = 6
DATES = 2
VMEM_BYTES = 8 * 2**20

TAIL = (
    -1.325748085975647,
    -1.8081518411636353,
    -0.41172587871551514,
    -0.042724475264549255,
    0.0027914412785321474,
    0.00040712140616960824,
    -0.00013435240543913096,
    1.5000393432273995e-05,
    -6.33199476851587e-07,
)


def iota(shape, dimension):
    return lax.broadcasted_iota(jnp.int32, shape, dimension)


def offsets(core):
    return [NEAR] + [jnp.where(core == 0, first, second) for first, second in FAR]


def slot_offsets(core):
    near, *far = offsets(core)
    *handed, last = offsets(1 - core)[1:]
    return [0, *far, *handed, near, last]


def pack(*refs):
    count_of = len(INPUTS)
    sources, outs = refs[:count_of], refs[count_of : count_of + 2 + len(FAR)]
    grid = refs[count_of + 2 + len(FAR)]
    held, arrived = refs[count_of + 3 + len(FAR) : -1], refs[-1]
    copies = [
        pltpu.make_async_copy(source, target, arrived.at[at])
        for at, (source, target) in enumerate(zip(sources, held))
    ]
    for copy in copies:
        copy.start()
    for at, rows in enumerate(curve_rows()):
        grid[at] = rows
    me, core = lax.axis_index("trade"), lax.axis_index("path")
    half = LANES // 2
    low = iota((SLOTS_TILE, LANES), 1) < half
    row, lane = iota((SLOTS_TILE, LANES), 0), iota((SLOTS_TILE, LANES), 1)
    for copy in copies:
        copy.wait()
    kind, start, count, strike, vol, notional, live, group, shocks = held
    own_shocks = jnp.zeros((SLOTS_TILE, LANES), jnp.float32)
    for factor in range(2):
        for date in range(DATES):
            value = jnp.broadcast_to(shocks[factor : factor + 1, date : date + 1], (SLOTS_TILE, LANES))
            own_shocks = jnp.where(lane == factor * DATES + date, value, own_shocks)
    for out, offset in zip(outs, [0] + offsets(core)):
        owner = me ^ offset
        cut = pl.ds(pl.multiple_of(owner // 2 * LANES, LANES), LANES)

        here = low == (owner % 2 == 0)

        def both(in_place, turned):
            return jnp.where(here, in_place, pltpu.roll(turned, half, 1))

        def field(ref):
            return both(ref[:SLOTS_TILE, cut], ref[SLOTS_TILE:, cut])

        lives = jnp.broadcast_to(live[:, cut], (SLOTS_TILE, LANES))
        sets = jnp.broadcast_to(group[:, cut], (SLOTS_TILE, LANES))
        slot = row + jnp.where(here, 0, SLOTS_TILE)
        first, kinds = field(start), field(kind)
        size = jnp.where(kinds == 2, 2.0, 1.0) * field(notional)
        tiles = (
            first.astype(jnp.float32),
            (first + field(count)).astype(jnp.float32),
            field(strike),
            field(vol),
            jnp.where(slot < both(lives, lives), size, 0.0),
            jnp.where(kinds == 1, 1.0, jnp.where(kinds == 2, 0.5, 0.0)),
            jnp.where(row == 0, (both(sets, sets) - owner * SET_DEV).astype(jnp.float32), own_shocks),
        )
        for at, tile in enumerate(tiles):
            out[at * SLOTS_TILE : (at + 1) * SLOTS_TILE, :] = tile
    outs[1][ROWS:, :] = jnp.zeros((SLOTS_TILE, LANES), jnp.float32)


def add_shocks(shocks, *refs):
    core = lax.axis_index("path")
    lane = iota((1, LANES), 1)
    line = jnp.zeros((1, LANES), jnp.float32)
    for factor in range(2):
        for date in range(DATES):
            value = jnp.broadcast_to(shocks[factor : factor + 1, date : date + 1], (1, LANES))
            line = jnp.where(lane == factor * DATES + date, value, line)
    for ref in refs[len(FAR) :]:
        ref[pl.ds(FIELDS * SLOTS_TILE + 2 - core, 1), :] = line


def split(values, count):
    parts = []
    for _ in range(count):
        part = values.astype(jnp.bfloat16)
        parts.append(part)
        values = values - part.astype(jnp.float32)
    return jnp.concatenate(parts, axis=0)


def add_parts(product, count):
    rows = product.shape[0] // count
    total = product[(count - 1) * rows :]
    for part in range(count - 2, -1, -1):
        total = total + product[part * rows : (part + 1) * rows]
    return total


def curve_rows():
    node = iota((SLOTS_TILE, GRID), 1).astype(jnp.float32) * YEAR_STEP
    row = iota((SLOTS_TILE, GRID), 0)
    valued = jnp.where(row < DATES + 1, row, 1).astype(jnp.float32) * YEAR_STEP
    horizon = node - valued
    front = -FLAT_RATE * horizon + 0.5 * (
        factor_variance(horizon) - factor_variance(node) + factor_variance(valued)
    )
    return front, loading(REVERT_FAST, horizon), loading(REVERT_SLOW, horizon)


def tables(shocks, grid):
    states = evolve(shocks)
    discounts = []
    for date in range(DATES):
        front, fast, slow = (grid[at, date + 1 : date + 2, :] for at in range(3))
        discounts.append(jnp.exp(front - fast * states[0, date] - slow * states[1, date]))
    both = jnp.concatenate(discounts, axis=0)
    mid = GRID // 4
    source, target = iota((GRID, GRID), 0), iota((GRID, GRID), 1)
    weights = jnp.where((source > mid) & (source <= target), YEAR_STEP, 0.0) - jnp.where(
        (source <= mid) & (source > target), YEAR_STEP, 0.0
    )
    sums = jnp.dot(split(both, 3), weights.astype(jnp.bfloat16), preferred_element_type=jnp.float32)
    return both, add_parts(sums, 3)


def price_source(ref, tables_of, slots):
    def field(at):
        return ref[at * SLOTS_TILE : (at + 1) * SLOTS_TILE, :]

    def look_up(table, at, index):
        row = jnp.broadcast_to(table[at : at + 1, :], (SLOTS_TILE, LANES))
        return jnp.take_along_axis(row, index, axis=1, mode="promise_in_bounds")

    def merge(first, second, bit):
        if first is None and second is None:
            return None
        zero = jnp.zeros((SLOTS_TILE, LANES), jnp.float32)
        first = zero if first is None else first
        second = zero if second is None else second
        mask = (iota((SLOTS_TILE, LANES), 0) & bit) == 0
        return jnp.where(mask, first, second) + pltpu.roll(jnp.where(mask, second, first), bit, 0)

    first, last = field(0), field(1)
    first_node, last_node = first.astype(jnp.int32), last.astype(jnp.int32)
    strike, vol, size, offset = field(2), field(3), field(4), field(5)
    tilt = 0.5 - offset
    totals = []
    for date in range(DATES):
        spread = vol * jnp.sqrt(first * YEAR_STEP - (date + 1) * YEAR_STEP)
        inverse = 1.0 / spread
        scale = size * spread
        hurdle = strike * inverse
        rows = [(*tables_of(slot), date * SLOTS + slot) for slot in slots]
        starts = [(look_up(curve, at, first_node), look_up(sums, at, first_node)) for curve, sums, at in rows]
        ends = [(look_up(curve, at, last_node), look_up(sums, at, last_node)) for curve, sums, at in rows]
        values = [None] * SLOTS
        for slot, (curve_start, sum_start), (curve_end, sum_end) in zip(slots, starts, ends):
            float_leg, annuity = curve_start - curve_end, sum_end - sum_start
            standard = float_leg * pl.reciprocal(annuity) * inverse - hurdle
            size_of = jnp.abs(standard)
            power = jnp.full_like(size_of, TAIL[-1])
            for term in TAIL[-2::-1]:
                power = power * size_of + term
            values[slot] = scale * annuity * (0.5 * size_of + tilt * standard + jnp.exp2(power))
        for bit in (1, 2, 4):
            values = [merge(a, b, bit) for a, b in zip(values[::2], values[1::2])]
        totals.append(values[0])
    return jnp.concatenate(totals, axis=0)


def set_tables(refs, grid, discount, running):
    line = FIELDS * SLOTS_TILE + 1 + lax.axis_index("path")
    empty = jnp.zeros((1, LANES), jnp.float32)
    lines = jnp.concatenate([empty if ref is None else ref[pl.ds(line, 1), :] for ref in refs], axis=0)
    shocks = [jnp.broadcast_to(lines[:, at : at + 1], (SLOTS, LANES)) for at in range(2 * DATES)]
    shocks = jnp.stack([jnp.stack(shocks[:DATES]), jnp.stack(shocks[DATES:])])
    discount[...], running[...] = tables(shocks, grid)


def net(refs, totals):
    extra = FIELDS * SLOTS_TILE
    set_index = iota((SET_DEV, LANES), 0).astype(jnp.float32)
    netted = None
    for group in range(0, len(refs), 4):
        cut = slice(group, group + 4)
        one_hot = jnp.concatenate(
            [(set_index == ref[extra : extra + 1, :]).astype(jnp.bfloat16) for ref in refs[cut]], axis=1
        )
        product = lax.dot_general(
            split(jnp.concatenate(totals[cut], axis=1), 3),
            one_hot,
            (((1,), (1,)), ((), ())),
            preferred_element_type=jnp.float32,
        )
        netted = product if netted is None else netted + product
    return add_parts(netted, 3)


def price_early(*refs):
    refs, (grid, out, discount, running) = refs[:-4], refs[-4:]
    set_tables([*refs, *[None] * (SLOTS - EARLY)], grid, discount, running)
    out[...] = net(refs, [price_source(ref, lambda slot: (discount, running), range(EARLY)) for ref in refs])


def price_late(*refs):
    refs, (grid, early, discount, running, out, late_discount, late_running) = refs[:-7], refs[-7:]
    set_tables([*[None] * EARLY, *refs[EARLY:]], grid, late_discount, late_running)

    def tables_of(slot):
        return (discount, running) if slot < EARLY else (late_discount, late_running)

    totals = [price_source(ref, tables_of, range(SLOTS)) for ref in refs[EARLY:]]
    totals = [price_source(ref, tables_of, range(EARLY, SLOTS)) for ref in refs[:EARLY]] + totals
    netted = jnp.maximum(net(refs, totals) + early[...], 0.0)
    me = lax.axis_index("trade")
    for slot, offset in enumerate(slot_offsets(lax.axis_index("path"))):
        for date in range(DATES):
            at = date * SLOTS + slot
            out[pl.ds(date * SLOTS + (me ^ offset), 1), :] = netted[at : at + 1, :]


def shards_by_trade(
    shocks, trade_kind, cash_start, cash_count, strike, normal_vol, notional, block_count, block_set
):
    dates_count = shocks.shape[1]
    own_shocks = shocks.reshape(2, dates_count)
    swap = [(0, 1), (1, 0)]
    other_shocks = lax.ppermute(shocks, "path", swap).reshape(2, dates_count)
    fields = (
        trade_kind.T,
        cash_start.T,
        cash_count.T,
        strike.T,
        normal_vol.T,
        notional.T,
        block_count.reshape(1, -1),
        block_set.reshape(1, -1),
        own_shocks,
    )
    message = jax.ShapeDtypeStruct((ROWS, LANES), jnp.float32)
    near_message = jax.ShapeDtypeStruct((ROWS + SLOTS_TILE, LANES), jnp.float32)
    limit = pltpu.CompilerParams(vmem_limit_bytes=VMEM_BYTES)
    own, near, *far, grid = pl.pallas_call(
        pack,
        out_shape=[message, near_message] + [message] * len(FAR) + [jax.ShapeDtypeStruct((3, SLOTS_TILE, GRID), jnp.float32)],
        in_specs=[pl.BlockSpec(memory_space=pltpu.HBM)] * len(fields),
        scratch_shapes=[pltpu.VMEM(field.shape, field.dtype) for field in fields]
        + [pltpu.SemaphoreType.DMA((len(fields),))],
        compiler_params=limit,
        name="pack",
    )(*(pltpu.with_memory_space_constraint(field, pltpu.HBM) for field in fields))
    owners = lax.axis_size("trade")
    near_in = lax.ppermute(near, "trade", [(at, at ^ NEAR) for at in range(owners)])
    far = pl.pallas_call(
        add_shocks,
        out_shape=[message] * len(FAR),
        input_output_aliases={1 + at: at for at in range(len(FAR))},
        compiler_params=limit,
        name="add_shocks",
    )(other_shocks, *far)
    far_in = []
    for piece, pair in zip(far, FAR):
        turns = [(2 * at + core, 2 * (at ^ pair[core]) + core) for at in range(owners) for core in range(2)]
        far_in.append(lax.ppermute(piece, ("trade", "path"), turns))
    handed = [lax.ppermute(piece, "path", swap) for piece in far_in]
    result = jax.ShapeDtypeStruct((dates_count * SLOTS, SET_DEV), jnp.float32)
    table = jax.ShapeDtypeStruct((dates_count * SLOTS, GRID), jnp.float32)
    slots = (own, *far_in, *handed[:-1], near_in, handed[-1])
    early = pl.pallas_call(
        price_early,
        out_shape=[result, table, table],
        compiler_params=limit,
        name="price_early",
    )(*slots[:EARLY], grid)
    netted = pl.pallas_call(
        price_late,
        out_shape=result,
        scratch_shapes=[pltpu.VMEM(table.shape, table.dtype)] * 2,
        compiler_params=limit,
        name="price_late",
    )(*slots, grid, *early)
    return netted.reshape(dates_count, SLOTS_TILE, SET_DEV).transpose(2, 0, 1)


def shards(shocks, trade_kind, *others):
    blocks, slot_count = trade_kind.shape
    by_trade = (
        lax.axis_size("trade") == SLOTS_TILE
        and lax.axis_size("path") == 2
        and shocks.shape == (2, DATES, 1, 1)
        and slot_count == 2 * SLOTS_TILE
        and blocks == SLOTS_TILE * LANES // 2
    )
    return (shards_by_trade if by_trade else shards_by_sum)(shocks, trade_kind, *others)


def solution(mesh):
    placed = (
        P("book", None, "path", "trade"),
        P(("book", "trade"), None),
        P(("book", "trade"), None),
        P(("book", "trade"), None),
        P(("book", "trade"), None),
        P(("book", "trade"), None),
        P(("book", "trade"), None),
        P(("book", "trade")),
        P(("book", "trade")),
    )
    return jax.shard_map(
        shards,
        mesh=mesh,
        in_specs=placed,
        out_specs=P(("book", "trade"), None, "path"),
        check_vma=False,
    )
```
